256 devices in a mesh: ctx: 32 (over y, x, core), head: 8 (over z).
Axes of the slice: x: 4, y: 4, z: 8, core: 2. Of those that a mesh axis runs over, the one named last changes fastest.
Arguments:
- queries: bfloat16 [4096, 8192], P('ctx', 'head'), parts along dimension 1, may hold values from -5 to 5
- keys: bfloat16 [4096, 1024], P('ctx', 'head'), parts along dimension 1, may hold values from -5 to 5
- values: bfloat16 [4096, 1024], P('ctx', 'head'), parts along dimension 1, may hold values from -6 to 6
- grad_out: bfloat16 [4096, 8192], P('ctx', 'head'), parts along dimension 1, may hold values from -6 to 6
- doc_lengths: int32 [4], replicated, may hold values from 1 to 2048, 4096 in all
- stretch_order: int32 [64], replicated, may hold values from 0 to 63, each once
Outputs:
- grad_queries: bfloat16 [4096, 8192], P('ctx', 'head'), parts along dimension 1
- grad_keys: bfloat16 [4096, 1024], P('ctx', 'head'), parts along dimension 1
- grad_values: bfloat16 [4096, 1024], P('ctx', 'head'), parts along dimension 1
The draws below stay inside these ranges and needn't reach their ends.
There are 8 independent parts, one for each index of `head`. The reference program is written for one: setup_inputs(seed, part) draws one part's arguments, and reference() takes and returns one part's arrays. A program takes and returns all parts, laid end to end along the dimension named above; an argument that names none is the same for every part. Nothing has to cross between parts.
Inputs may be any that keep to these rules, and one draw needn't show every extreme that they name: `doc_lengths`: the lengths sum to 4096; the longest is exactly 2048. `stretch_order`: each stretch number appears exactly once.
All inputs are finite; a program needn't handle non-finite values.
Results may differ from the reference program's by a relative error of at most 0.018.
Values may be sent and summed in bfloat16 or wider, within the bound.
A program may use at most 64 MiB of HBM per device.

```python
import math
import jax
import jax.numpy as jnp
import numpy as np
from jax import lax

HEADS = 8
HEAD_DIM = 128
TOK_DEV = 128
NDOC = 4
TOKENS = 4096
N_CTX = 32


def draw_queries(key, part):
    key = jax.random.fold_in(key, 1)
    values_drawn = jnp.clip(jax.random.normal(key, (TOKENS, HEADS * HEAD_DIM)), -4.5, 4.5)
    return values_drawn.astype(jnp.bfloat16)


def draw_keys(key, part):
    key = jax.random.fold_in(key, 2)
    values_drawn = jnp.clip(jax.random.normal(key, (TOKENS, HEAD_DIM)), -4.5, 4.5)
    return values_drawn.astype(jnp.bfloat16)


def levels(rng, dims, split, low, largest):
    def one(axis_at, parts):
        heights = jax.random.uniform(jax.random.fold_in(jax.random.fold_in(rng, 6), axis_at), (parts,), jnp.float32, low / len(split), largest / len(split))
        return jnp.repeat(jnp.exp(heights), dims[axis_at] // parts).reshape((-1,) + (1,) * (len(dims) - axis_at - 1))

    level = one(*split[0])
    for cut in split[1:]:
        level = level * one(*cut)
    return level


def length_profile(count, total, limit, skew):
    loads = [(1 << 20) // math.isqrt(standing ** skew) + 1 for standing in range(2, count + 1)]
    rest, counts = total - limit - (count - 1), [1] * (count - 1)
    while rest > 0:
        candidates = [i for i in range(count - 1) if counts[i] < limit]
        mass, left = sum([loads[i] for i in candidates]), rest
        for i in candidates:
            addition = min(limit - counts[i], max(1, left * loads[i] // mass), rest)
            counts[i] = counts[i] + addition
            rest = rest - addition
    return np.array([limit] + counts)


def uneven_parts(stream_key, count, total, limit, slope):
    if count == 2:
        one = jax.random.randint(stream_key, (), max(1, total - limit), min(limit, total - 1) + 1)
        return jnp.stack([one, total - one])
    sizes = jnp.asarray(length_profile(count, total, limit, slope), jnp.int32)
    twos = (count - 1) // 2
    giver, sink = sizes[1:1 + 2 * twos:2], sizes[2:2 + 2 * twos:2]
    room = jnp.minimum(giver - 1, limit - sink)
    shifted = jax.random.randint(jax.random.fold_in(stream_key, 1), (twos,), 0, 1 << 20) % (room + 1)
    sizes = sizes.at[1:1 + 2 * twos:2].set(giver - shifted).at[2:2 + 2 * twos:2].set(sink + shifted)
    return sizes[jax.random.permutation(jax.random.fold_in(stream_key, 2), count)]


def normal_values(stream_key, extent, spread, limit, shards=(), kind=jnp.bfloat16):
    loudness = levels(stream_key, extent, shards, -0.22, 0.18) if shards else 1.0
    drawn = jax.random.normal(stream_key, extent, jnp.float32) * spread * loudness
    return jnp.minimum(jnp.maximum(drawn, -limit), limit).astype(kind)


def setup_inputs(seed: int = 0, part: int = 0) -> dict:
    key_of = jax.random.split(jax.random.key(seed), 7)
    part_keys = jax.random.split(jax.random.fold_in(key_of[6], part), 7)
    return {
        "queries": draw_queries(jax.random.fold_in(jax.random.fold_in(key_of[6], part), 71), part),
        "keys": draw_keys(jax.random.fold_in(jax.random.fold_in(key_of[6], part), 71), part),
        "values": normal_values(part_keys[2], (TOKENS, HEAD_DIM), 1.0, 6.0, ((0, 32),)),
        "grad_out": normal_values(part_keys[3], (TOKENS, HEADS * HEAD_DIM), 1.0, 6.0, ((0, 32),)),
        "doc_lengths": uneven_parts(key_of[4], NDOC, TOKENS, TOKENS // 2, 2).astype(jnp.int32),
        "stretch_order": jax.random.permutation(key_of[5], 2 * N_CTX).astype(jnp.int32),
    }


def token_positions(stretch_order, row_count, stretch_rows):
    row_index = jnp.arange(row_count, dtype=jnp.int32)
    return (stretch_order[row_index // stretch_rows] * stretch_rows + row_index % stretch_rows).astype(jnp.int32)


def span_starts(doc_lengths, positions):
    starts = (jnp.cumsum(doc_lengths) - doc_lengths).astype(jnp.int32)
    inside = starts[None, :] <= positions[:, None]
    return jnp.max(jnp.where(inside, starts[None, :], 0), axis=1).astype(jnp.int32)


def reference(queries, keys, values, grad_out, doc_lengths, stretch_order):
    stretch_rows = TOK_DEV // 2
    scaling = HEAD_DIM ** -0.5
    positions = token_positions(stretch_order, TOKENS, stretch_rows)
    span_first = span_starts(doc_lengths, positions)
    key_wide = keys.astype(jnp.float32)
    value_wide = values.astype(jnp.float32)

    def shard_step(running, shard_index):
        grad_k, grad_v = running
        first_row = (shard_index * TOK_DEV).astype(jnp.int32)
        query_part = lax.dynamic_slice_in_dim(queries, first_row, TOK_DEV, 0).astype(jnp.float32).reshape(TOK_DEV, HEADS, HEAD_DIM)
        grad_part = lax.dynamic_slice_in_dim(grad_out, first_row, TOK_DEV, 0).astype(jnp.float32).reshape(TOK_DEV, HEADS, HEAD_DIM)
        query_pos = lax.dynamic_slice_in_dim(positions, first_row, TOK_DEV, 0)
        query_first = lax.dynamic_slice_in_dim(span_first, first_row, TOK_DEV, 0)
        allowed = (positions[None, :] <= query_pos[:, None]) & (positions[None, :] >= query_first[:, None])
        scores = jnp.einsum("rhd,kd->hrk", query_part, key_wide) * scaling
        row_max = jnp.max(jnp.where(allowed[None], scores, -jnp.inf), axis=2)
        row_sum = jnp.sum(jnp.where(allowed[None], jnp.exp(scores - row_max[:, :, None]), 0.0), axis=2)
        log_norm = row_max + jnp.log(row_sum)
        weights = jnp.where(allowed[None], jnp.exp(scores - log_norm[:, :, None]), 0.0)
        weights_low = lax.optimization_barrier(weights.astype(jnp.bfloat16)).astype(jnp.float32)
        attended = jnp.einsum("hrk,kd->hrd", weights_low, value_wide)
        row_delta = jnp.einsum("rhd,hrd->hr", grad_part, attended)
        grad_weights = jnp.einsum("rhd,kd->hrk", grad_part, value_wide)
        grad_scores = weights * (grad_weights - row_delta[:, :, None])
        grad_scores = lax.optimization_barrier(grad_scores.astype(jnp.bfloat16)).astype(jnp.float32)
        grad_q = jnp.einsum("hrk,kd->rhd", grad_scores, key_wide) * scaling
        grad_q = grad_q.astype(jnp.bfloat16).reshape(TOK_DEV, HEADS * HEAD_DIM)
        grad_k = grad_k + jnp.einsum("hrk,rhd->kd", grad_scores, query_part) * scaling
        grad_v = grad_v + jnp.einsum("hrk,rhd->kd", weights_low, grad_part)
        return (grad_k, grad_v), grad_q

    empty_grads = jnp.zeros((TOKENS, HEAD_DIM), jnp.float32)
    (grad_k, grad_v), grad_q = lax.scan(shard_step, (empty_grads, empty_grads), jnp.arange(N_CTX, dtype=jnp.int32))
    return grad_q.reshape(TOKENS, HEADS * HEAD_DIM), grad_k.astype(jnp.bfloat16), grad_v.astype(jnp.bfloat16)
```

```python
import functools

import jax
import jax.numpy as jnp
from jax import lax
from jax.experimental import pallas as pl
from jax.experimental.pallas import tpu as pltpu
from jax.sharding import PartitionSpec as P

MESH = pl.DeviceIdType.MESH
F32, BF16 = jnp.float32, jnp.bfloat16
RING = 4
HEADS, DIM = 8, 128
STRETCH = 64
STRETCHES = 64
COLS = HEADS * STRETCH
WIN = 34
WROWS = WIN * STRETCH
KC = 1088
NEG = -1e30
N_AG = 64
N_RS = 32


def dot_nt(a, b):
    return lax.dot_general(a, b, (((1,), (1,)), ((), ())), preferred_element_type=F32)


def dot_nn(a, b):
    return lax.dot_general(a, b, (((1,), (0,)), ((), ())), preferred_element_type=F32)


def fold8(v, op):
    parts = v.reshape(v.shape[0] // 8, 8, v.shape[1])
    return op(parts, axis=0)


def kernel(
    q_hbm, k_hbm, v_hbm, g_hbm, len_ref, ord_ref, inv_ref,
    dq_ref, dk_ref, dv_ref,
    gkv, q_in, g_in, q_s, g_s, qn_s, gn_s, ksw, vsw, ktw, sbuf, pbuf, dsbuf, dkw, dvw,
    part_a, part_b, pair_a, pair_b, s0_a, s0_b, r1_a, r1_b, s1_a, s1_b, r2_a, r2_b,
    loc_sem, ag_send, ag_recv, rs_send, rs_recv,
):
    me = lax.axis_index("ctx")
    head = lax.axis_index("head")
    c = lax.rem(me, 2)
    x = lax.rem(lax.div(me, 2), RING)
    y = lax.div(me, 2 * RING)
    oc = 1 - c

    def wrap(v):
        return lax.rem(v + RING, RING)

    x1, x2, x3 = wrap(x + 1), wrap(x + 2), wrap(x + 3)
    y1, y2, y3 = wrap(y + 1), wrap(y + 2), wrap(y + 3)

    def dev(yy, xx, cc):
        return ((yy * RING + xx) * 2 + cc, head)

    right, left = dev(y, x1, c), dev(y, x3, c)
    up, down = dev(y1, x, c), dev(y3, x, c)
    sib = dev(y, x, oc)

    loads = [
        pltpu.make_async_copy(q_hbm, q_in, loc_sem.at[0]),
        pltpu.make_async_copy(g_hbm, g_in, loc_sem.at[1]),
    ]
    own = []
    for h in range(2):
        rows = pl.ds(h * STRETCH, STRETCH)
        own.append(pltpu.make_async_copy(k_hbm.at[rows], gkv.at[2 * me + h, 0], loc_sem.at[2 + 2 * h]))
        own.append(pltpu.make_async_copy(v_hbm.at[rows], gkv.at[2 * me + h, 1], loc_sem.at[3 + 2 * h]))
    for cp in own + loads:
        cp.start()

    barrier = pltpu.get_barrier_semaphore()
    for peer in (right, left, up, down, sib):
        pl.semaphore_signal(barrier, inc=1, device_id=peer, device_id_type=MESH)
    pl.semaphore_wait(barrier, 5)
    for cp in own:
        cp.wait()

    sent = []
    state = {"n": 0}

    def new_slot():
        state["n"] += 1
        return state["n"] - 1

    def send(ref, k, to):
        cp = pltpu.make_async_remote_copy(
            src_ref=ref, dst_ref=ref, send_sem=ag_send.at[k], recv_sem=ag_recv.at[k],
            device_id=to, device_id_type=MESH,
        )
        cp.start()
        sent.append(cp)

    def arrive(ref, k):
        pltpu.make_async_remote_copy(
            src_ref=ref, dst_ref=ref, send_sem=ag_send.at[k], recv_sem=ag_recv.at[k],
            device_id=sib, device_id_type=MESH,
        ).wait_recv()

    def first_block(yy, xx, cc):
        return ((yy * RING + xx) * 2 + cc) * 2

    def node(yy, xx, cc=None):
        return gkv.at[pl.ds(first_block(yy, xx, c if cc is None else cc), 2)]

    def sides_of(yy, xx, side):
        return gkv.at[pl.ds(first_block(yy, xx, c), 2), side]

    def half_of(yy, xx, cc, half):
        return gkv.at[first_block(yy, xx, cc) + half]

    def quarter(yy, xx, half, side):
        return gkv.at[first_block(yy, xx, c) + half, side]

    sib_waits = []

    def to_sib(cut):
        k = new_slot()
        send(cut(c), k, sib)
        sib_waits.append((cut(oc), k))

    mine = node(y, x)
    k_r, k_l, k_u, k_d = new_slot(), new_slot(), new_slot(), new_slot()
    send(mine, k_r, right)
    send(mine, k_l, left)
    send(mine, k_u, up)
    send(mine, k_d, down)
    to_sib(lambda cc: node(y, x, cc))

    lo, hi = 0, 1
    far = {}
    second = []

    def first_hop(k, yy, xx, along, opposite, side, half, sides, tag):
        arrive(node(yy, xx), k)
        kf = new_slot()
        send(sides_of(yy, xx, side), kf, opposite)
        far[tag] = kf
        ks_ = []
        for to in sides:
            kk = new_slot()
            send(half_of(yy, xx, c, half), kk, to)
            ks_.append(kk)
        to_sib(lambda cc: node(yy, xx, cc))
        return ks_

    def opp_slots(names):
        return names

    from_l = first_hop(k_r, y, x3, None, right, lo, 0, (up, down), "xl")
    from_r = first_hop(k_l, y, x1, None, left, hi, 0, (up, down), "xr")
    from_d = first_hop(k_u, y3, x, None, up, lo, 1, (right, left), "yd")
    from_u = first_hop(k_d, y1, x, None, down, hi, 1, (right, left), "yu")

    arrive(sides_of(y, x2, lo), far["xl"])
    arrive(sides_of(y, x2, hi), far["xr"])
    xf = []
    for to in (up, down):
        kk = new_slot()
        send(half_of(y, x2, c, 0), kk, to)
        xf.append(kk)
    to_sib(lambda cc: node(y, x2, cc))
    arrive(sides_of(y2, x, lo), far["yd"])
    arrive(sides_of(y2, x, hi), far["yu"])
    yf = []
    for to in (right, left):
        kk = new_slot()
        send(half_of(y2, x, c, 1), kk, to)
        yf.append(kk)
    to_sib(lambda cc: node(y2, x, cc))

    last = []

    def second_hop(k, yy, xx, half, side, to, fy, fx):
        arrive(half_of(yy, xx, c, half), k)
        kk = new_slot()
        send(quarter(yy, xx, half, side), kk, to)
        to_sib(lambda cc: half_of(yy, xx, cc, half))
        return kk

    for xx, slots in ((x3, from_l), (x1, from_r), (x2, xf)):
        ka = second_hop(slots[0], y3, xx, 0, lo, up, y2, xx)
        kb = second_hop(slots[1], y1, xx, 0, hi, down, y2, xx)
        last.append((y2, xx, 0, ka, kb))
    for yy, slots in ((y3, from_d), (y1, from_u), (y2, yf)):
        ka = second_hop(slots[0], yy, x3, 1, lo, right, yy, x2)
        kb = second_hop(slots[1], yy, x1, 1, hi, left, yy, x2)
        last.append((yy, x2, 1, ka, kb))
    for yy, xx, half, ka, kb in last:
        arrive(quarter(yy, xx, half, lo), ka)
        arrive(quarter(yy, xx, half, hi), kb)
        to_sib(lambda cc, yy=yy, xx=xx, half=half: half_of(yy, xx, cc, half))

    for cp in loads:
        cp.wait()
    for a in range(2):
        for h in range(HEADS):
            src = (pl.ds(a * STRETCH, STRETCH), pl.ds(h * DIM, DIM))
            q_s[a, pl.ds(h * STRETCH, STRETCH), :] = q_in[src]
            g_s[a, pl.ds(h * STRETCH, STRETCH), :] = g_in[src]

    for ref, k in sib_waits:
        arrive(ref, k)

    spots, base = [], []
    for a in range(2):
        p = ord_ref[2 * me + a]
        spots.append(p)
        base.append(jnp.maximum(lax.div(p, 2) * 2 - 32, 0))

    def window_step(w, carry):
        rows = pl.ds(pl.multiple_of(w * STRETCH, STRETCH), STRETCH)
        for a in range(2):
            b = inv_ref[base[a] + w]
            ksw[a, rows, :] = gkv[b, 0]
            vsw[a, rows, :] = gkv[b, 1]
        return carry

    lax.fori_loop(0, WIN, window_step, 0)

    def turn_step(j, carry):
        rows = pl.ds(pl.multiple_of(j * 128, 128), 128)
        for a in range(2):
            ktw[a, :, rows] = ksw[a, rows, :].T
        return carry

    lax.fori_loop(0, WIN // 2, turn_step, 0)

    scale = DIM ** -0.5
    log2e = 1.4426950408889634
    starts = [jnp.int32(0)]
    for d in range(3):
        starts.append(starts[-1] + len_ref[d])
    lane = lax.broadcasted_iota(jnp.int32, (1, 128), 1)
    row_in = jnp.where(lane >= STRETCH, lane - STRETCH, lane)
    pos_row, first_row = [], []
    for a in range(2):
        pr = spots[a] * STRETCH + row_in
        fr = jnp.zeros_like(pr)
        for st in starts:
            fr = jnp.maximum(fr, jnp.where(st <= pr, st, 0))
        pos_row.append(pr)
        first_row.append(fr)

    groups = COLS // 128

    def score_step(j, carry):
        new = []
        for a in range(2):
            s = dot_nt(ksw[a, pl.ds(pl.multiple_of(j * KC, 16), KC), :], q_s[a])
            first_key = base[a] * STRETCH + j * KC
            kpos = first_key + lax.broadcasted_iota(jnp.int32, (KC, 128), 0)
            ok = (kpos <= pos_row[a]) & (kpos >= first_row[a])
            for g in range(groups):
                cols = pl.ds(g * 128, 128)
                sg = jnp.where(ok, s[:, g * 128:(g + 1) * 128] * (scale * log2e), NEG)
                sbuf[a, pl.ds(pl.multiple_of(j * KC, 8), KC), cols] = sg
                new.append(jnp.maximum(carry[a * groups + g], fold8(sg, jnp.max)))
        return tuple(new)

    tops = lax.fori_loop(
        0, WROWS // KC, score_step, tuple(jnp.full((8, 128), NEG, F32) for _ in range(2 * groups))
    )
    tops = [jnp.max(t, axis=0, keepdims=True) for t in tops]

    def weight_step(j, carry):
        new = []
        rows = pl.ds(pl.multiple_of(j * KC, 16), KC)
        for a in range(2):
            dp = dot_nt(vsw[a, rows, :], g_s[a])
            for g in range(groups):
                cols = pl.ds(g * 128, 128)
                pw = jnp.exp2(sbuf[a, rows, cols] - tops[a * groups + g])
                dpg = dp[:, g * 128:(g + 1) * 128]
                pbuf[a, rows, cols] = pw.astype(BF16)
                sbuf[a, rows, cols] = dpg
                total, dsum = carry[a * groups + g]
                new.append((total + fold8(pw, jnp.sum), dsum + fold8(pw * dpg, jnp.sum)))
        return tuple(new)

    zero = jnp.zeros((8, 128), F32)
    sums = lax.fori_loop(
        0, WROWS // KC, weight_step, tuple((zero, zero) for _ in range(2 * groups))
    )
    inv_l, delta = [], []
    for total, dsum in sums:
        r = 1.0 / jnp.sum(total, axis=0, keepdims=True)
        inv_l.append(r)
        delta.append(jnp.sum(dsum, axis=0, keepdims=True) * r)

    for a in range(2):
        for g in range(groups):
            rows = pl.ds(g * 128, 128)
            col = jnp.broadcast_to(inv_l[a * groups + g], (128, 128)).T
            qn_s[a, rows, :] = (q_s[a, rows, :].astype(F32) * (col * scale)).astype(BF16)
            gn_s[a, rows, :] = (g_s[a, rows, :].astype(F32) * col).astype(BF16)

    def grad_step(j, carry):
        rows = pl.ds(pl.multiple_of(j * KC, 16), KC)
        for a in range(2):
            for g in range(groups):
                cols = pl.ds(g * 128, 128)
                pw = pbuf[a, rows, cols].astype(F32)
                dsbuf[a, rows, cols] = (pw * (sbuf[a, rows, cols] - delta[a * groups + g])).astype(BF16)
            spans = pl.ds(j * (KC // STRETCH), KC // STRETCH)
            wide = (KC // STRETCH, STRETCH, DIM)
            dvw[a, spans] = dot_nn(pbuf[a, rows, :], gn_s[a]).reshape(wide)
            dkw[a, spans] = dot_nn(dsbuf[a, rows, :], qn_s[a]).reshape(wide)
        return carry

    lax.fori_loop(0, WROWS // KC, grad_step, 0)
    for a in range(2):
        dkw[a, WIN] = jnp.zeros((STRETCH, DIM), F32)
        dvw[a, WIN] = jnp.zeros((STRETCH, DIM), F32)

    def unsort(cc, i):
        yy, xx = lax.div(i, RING), lax.rem(i, RING)
        for half, out in ((0, part_a.at[cc, xx]), (1, part_b.at[cc, yy])):
            s = ord_ref[2 * (2 * i + cc) + half]
            at = []
            for a in range(2):
                off = s - base[a]
                at.append(jnp.where((off >= 0) & (off < WIN), off, WIN))
            for kv, w in ((0, dkw), (1, dvw)):
                both = w[0, at[0]] + w[1, at[1]]
                other = yy if half == 0 else xx
                out[kv, other] = both.astype(BF16)

    def rs_copy(src, dst, k, to):
        return pltpu.make_async_remote_copy(
            src_ref=src, dst_ref=dst, send_sem=rs_send.at[k], recv_sem=rs_recv.at[k],
            device_id=to, device_id_type=MESH,
        )

    lax.fori_loop(0, RING * RING, lambda i, z: (unsort(oc, i), z)[1], 0)
    swap_a = rs_copy(part_a.at[oc], pair_a, 0, sib)
    swap_b = rs_copy(part_b.at[oc], pair_b, 1, sib)
    swap_a.start()
    swap_b.start()
    lax.fori_loop(0, RING * RING, lambda i, z: (unsort(c, i), z)[1], 0)

    swap_a.wait()
    swap_b.wait()

    def pair_step(i, carry):
        for part, pair, out in ((part_a, pair_a, s0_a), (part_b, pair_b, s0_b)):
            for kv in range(2):
                out[i, kv] = (part[c, i, kv].astype(F32) + pair[i, kv].astype(F32)).astype(BF16)
        return carry

    lax.fori_loop(0, RING, pair_step, 0)

    def ring_start(buf, recv, k0, p1, p2, p3, fwd, bwd):
        cps = [
            rs_copy(buf.at[p2, 0], recv.at[0], k0, fwd),
            rs_copy(buf.at[p2, 1], recv.at[1], k0 + 1, bwd),
            rs_copy(buf.at[p1, 1], recv.at[2], k0 + 2, fwd),
            rs_copy(buf.at[p3, 0], recv.at[3], k0 + 3, bwd),
        ]
        for cp in cps:
            cp.start()
        return cps

    def ring_mid(buf, recv, k0, p1, p2, p3, fwd, bwd, cps):
        cps[0].wait_recv()
        buf[p1, 0] = (buf[p1, 0].astype(F32) + recv[0].astype(F32)).astype(BF16)
        cp = rs_copy(buf.at[p1, 0], recv.at[4], k0 + 4, fwd)
        cp.start()
        cps.append(cp)
        cps[1].wait_recv()
        buf[p3, 1] = (buf[p3, 1].astype(F32) + recv[1].astype(F32)).astype(BF16)
        cp = rs_copy(buf.at[p3, 1], recv.at[5], k0 + 5, bwd)
        cp.start()
        cps.append(cp)

    def ring_end(buf, recv, at, cps):
        for i in range(2, 6):
            cps[i].wait_recv()
        k_sum = buf[at, 0].astype(F32) + recv[3].astype(F32) + recv[4].astype(F32)
        v_sum = buf[at, 1].astype(F32) + recv[2].astype(F32) + recv[5].astype(F32)
        return k_sum.astype(BF16), v_sum.astype(BF16)

    xs, ys = (x1, x2, x3, right, left), (y1, y2, y3, up, down)
    ca = ring_start(s0_a, r1_a, 2, *xs)
    cb = ring_start(s0_b, r1_b, 8, *ys)

    for a in range(2):
        dqt = dot_nn(ktw[a], dsbuf[a])
        for g in range(groups):
            block = (dqt[:, g * 128:(g + 1) * 128] * (inv_l[a * groups + g] * scale)).T.astype(BF16)
            for i in range(2):
                dq_ref[pl.ds(a * STRETCH, STRETCH), pl.ds((2 * g + i) * DIM, DIM)] = block[i * STRETCH:(i + 1) * STRETCH]

    ring_mid(s0_a, r1_a, 2, *xs, ca)
    ring_mid(s0_b, r1_b, 8, *ys, cb)
    k_sum, v_sum = ring_end(s0_a, r1_a, x, ca)
    for i in range(RING):
        s1_a[i, 0] = k_sum[i]
        s1_a[i, 1] = v_sum[i]
    ca2 = ring_start(s1_a, r2_a, 14, *ys)
    k_sum, v_sum = ring_end(s0_b, r1_b, y, cb)
    for i in range(RING):
        s1_b[i, 0] = k_sum[i]
        s1_b[i, 1] = v_sum[i]
    cb2 = ring_start(s1_b, r2_b, 20, *xs)
    ring_mid(s1_a, r2_a, 14, *ys, ca2)
    ring_mid(s1_b, r2_b, 20, *xs, cb2)
    k_sum, v_sum = ring_end(s1_a, r2_a, y, ca2)
    dk_ref[pl.ds(0, STRETCH), :] = k_sum
    dv_ref[pl.ds(0, STRETCH), :] = v_sum
    k_sum, v_sum = ring_end(s1_b, r2_b, x, cb2)
    dk_ref[pl.ds(STRETCH, STRETCH), :] = k_sum
    dv_ref[pl.ds(STRETCH, STRETCH), :] = v_sum

    for cp in sent + ca + cb + ca2 + cb2:
        cp.wait_send()


def body(queries, keys, values, grad_out, doc_lengths, stretch_order):
    slots = jnp.arange(STRETCHES, dtype=jnp.int32)
    inverse = jnp.sum(
        jnp.where(stretch_order[None, :] == slots[:, None], slots[None, :], 0), axis=1, dtype=jnp.int32
    )
    anyspec = pl.BlockSpec(memory_space=pl.ANY)
    smem = pl.BlockSpec(memory_space=pltpu.SMEM)
    vmem = pl.BlockSpec(memory_space=pltpu.VMEM)
    half = (STRETCH, DIM)
    return pl.pallas_call(
        kernel,
        out_shape=(
            jax.ShapeDtypeStruct(queries.shape, BF16),
            jax.ShapeDtypeStruct(keys.shape, BF16),
            jax.ShapeDtypeStruct(values.shape, BF16),
        ),
        in_specs=[anyspec] * 4 + [smem] * 3,
        out_specs=(vmem, vmem, vmem),
        scratch_shapes=[
            pltpu.VMEM((STRETCHES, 2) + half, BF16),
            pltpu.VMEM((2 * STRETCH, HEADS * DIM), BF16),
            pltpu.VMEM((2 * STRETCH, HEADS * DIM), BF16),
            pltpu.VMEM((2, COLS, DIM), BF16),
            pltpu.VMEM((2, COLS, DIM), BF16),
            pltpu.VMEM((2, COLS, DIM), BF16),
            pltpu.VMEM((2, COLS, DIM), BF16),
            pltpu.VMEM((2, WROWS, DIM), BF16),
            pltpu.VMEM((2, WROWS, DIM), BF16),
            pltpu.VMEM((2, DIM, WROWS), BF16),
            pltpu.VMEM((2, WROWS, COLS), F32),
            pltpu.VMEM((2, WROWS, COLS), BF16),
            pltpu.VMEM((2, WROWS, COLS), BF16),
            pltpu.VMEM((2, WIN + 1) + half, F32),
            pltpu.VMEM((2, WIN + 1) + half, F32),
            pltpu.VMEM((2, RING, 2, RING) + half, BF16),
            pltpu.VMEM((2, RING, 2, RING) + half, BF16),
            pltpu.VMEM((RING, 2, RING) + half, BF16),
            pltpu.VMEM((RING, 2, RING) + half, BF16),
            pltpu.VMEM((RING, 2, RING) + half, BF16),
            pltpu.VMEM((RING, 2, RING) + half, BF16),
            pltpu.VMEM((6, RING) + half, BF16),
            pltpu.VMEM((6, RING) + half, BF16),
            pltpu.VMEM((RING, 2) + half, BF16),
            pltpu.VMEM((RING, 2) + half, BF16),
            pltpu.VMEM((6,) + half, BF16),
            pltpu.VMEM((6,) + half, BF16),
            pltpu.SemaphoreType.DMA((6,)),
            pltpu.SemaphoreType.DMA((N_AG,)),
            pltpu.SemaphoreType.DMA((N_AG,)),
            pltpu.SemaphoreType.DMA((N_RS,)),
            pltpu.SemaphoreType.DMA((N_RS,)),
        ],
        compiler_params=pltpu.CompilerParams(
            collective_id=0, has_side_effects=True, vmem_limit_bytes=56 * 1024 * 1024
        ),
    )(queries, keys, values, grad_out, doc_lengths, stretch_order, inverse)


def solution(mesh):
    return jax.shard_map(
        body,
        mesh=mesh,
        in_specs=(P("ctx", "head"), P("ctx", "head"), P("ctx", "head"), P("ctx", "head"), P(), P()),
        out_specs=(P("ctx", "head"), P("ctx", "head"), P("ctx", "head")),
        check_vma=False,
    )
```

```python
import functools

import jax
import jax.numpy as jnp
from jax import lax
from jax.experimental import pallas as pl
from jax.experimental.pallas import tpu as pltpu
from jax.sharding import PartitionSpec as P

MESH = pl.DeviceIdType.MESH
F32, BF16 = jnp.float32, jnp.bfloat16
RING = 4
CHIPS = RING * RING
HEADS, DIM = 8, 128
STRETCH = 64
STRETCHES = 64
COLS = HEADS * STRETCH
GROUPS = COLS // 128
WIN = 34
WROWS = WIN * STRETCH
KC = 1088
NEG = -1e30
N_AG = 128
N_RS = 48


def dot_nt(a, b):
    return lax.dot_general(a, b, (((1,), (1,)), ((), ())), preferred_element_type=F32)


def dot_nn(a, b):
    return lax.dot_general(a, b, (((1,), (0,)), ((), ())), preferred_element_type=F32)


def fold8(v, op):
    return op(v.reshape(v.shape[0] // 8, 8, v.shape[1]), axis=0)


def kernel(
    q_hbm, k_hbm, v_hbm, g_hbm, len_ref, ord_ref,
    dq_ref, dk_ref, dv_ref,
    gk, gv, q_in, g_in, q_s, g_s, qn_s, gn_s, ksw, vsw, ktw, sbuf, pbuf, dsbuf, dkw, dvw,
    part_k, part_v, pair_k, pair_v, sum_k, sum_v, got_k, got_v, inv_vec, inv_ref,
    loc_sem, ag_send, ag_recv, rs_send, rs_recv,
):
    me = lax.axis_index("ctx")
    head = lax.axis_index("head")
    c = lax.rem(me, 2)
    x = lax.rem(lax.div(me, 2), RING)
    y = lax.div(me, 2 * RING)
    oc = 1 - c

    def wrap(v):
        return lax.rem(v, RING)

    xs = [wrap(x + d) for d in range(RING)]
    ys = [wrap(y + d) for d in range(RING)]

    def dev(yy, xx, cc):
        return ((yy * RING + xx) * 2 + cc, head)

    sib = dev(y, x, oc)

    own = []
    for i, (src, dst) in enumerate(((k_hbm, gk), (v_hbm, gv))):
        for h in range(2):
            rows = pl.ds(h * STRETCH, STRETCH)
            own.append(pltpu.make_async_copy(src.at[rows], dst.at[2 * me + h], loc_sem.at[2 * i + h]))
    loads = [
        pltpu.make_async_copy(q_hbm, q_in, loc_sem.at[4]),
        pltpu.make_async_copy(g_hbm, g_in, loc_sem.at[5]),
    ]
    for cp in own + loads:
        cp.start()

    barrier = pltpu.get_barrier_semaphore()
    peers = [dev(y, xs[d], c) for d in (1, 2, 3)] + [dev(ys[d], x, c) for d in (1, 2, 3)] + [sib]
    for peer in peers:
        pl.semaphore_signal(barrier, inc=1, device_id=peer, device_id_type=MESH)
    pl.semaphore_wait(barrier, len(peers))

    sent = []
    count = [0]

    def send(ref, to):
        k = count[0]
        count[0] += 1
        cp = pltpu.make_async_remote_copy(
            src_ref=ref, dst_ref=ref, send_sem=ag_send.at[k], recv_sem=ag_recv.at[k],
            device_id=to, device_id_type=MESH,
        )
        cp.start()
        sent.append(cp)
        return k

    def arrive(ref, k):
        pltpu.make_async_remote_copy(
            src_ref=ref, dst_ref=ref, send_sem=ag_send.at[k], recv_sem=ag_recv.at[k],
            device_id=sib, device_id_type=MESH,
        ).wait_recv()

    def block(yy, xx, cc):
        return ((yy * RING + xx) * 2 + cc) * 2

    def node(buf, yy, xx, cc):
        return buf.at[pl.ds(block(yy, xx, cc), 2)]

    def part_of(buf, yy, xx, cc, half):
        return buf.at[block(yy, xx, cc) + half]

    far_first, near_first = (2, 1, 3), (1, 3, 2)

    def first_stage(buf):
        mine = node(buf, y, x, c)
        along_x = {d: send(mine, dev(y, xs[d], c)) for d in far_first}
        along_y = {d: send(mine, dev(ys[d], x, c)) for d in far_first}
        return along_x, along_y, [(node(buf, y, x, oc), send(mine, sib))]

    def second_stage(buf, along_x, along_y, pending):
        coming = []
        for d in near_first:
            xx, yy = xs[RING - d], ys[RING - d]
            arrive(node(buf, y, xx, c), along_x[d])
            for e in far_first:
                k = send(part_of(buf, y, xx, c, 0), dev(ys[e], x, c))
                coming.append((e, ys[RING - e], xx, 0, k))
            arrive(node(buf, yy, x, c), along_y[d])
            for e in far_first:
                k = send(part_of(buf, yy, x, c, 1), dev(y, xs[e], c))
                coming.append((e, yy, xs[RING - e], 1, k))
            pending.append((node(buf, y, xx, oc), send(node(buf, y, xx, c), sib)))
            pending.append((node(buf, yy, x, oc), send(node(buf, yy, x, c), sib)))
        return coming

    def third_stage(buf, coming, pending):
        for e in near_first:
            for ee, yy, xx, half, k in coming:
                if ee == e:
                    arrive(part_of(buf, yy, xx, c, half), k)
                    pending.append((part_of(buf, yy, xx, oc, half), send(part_of(buf, yy, xx, c, half), sib)))

    lane = lax.broadcasted_iota(jnp.int32, (8, 128), 1)

    def invert_order():
        inv = jnp.zeros((8, 128), jnp.int32)
        for b in range(STRETCHES):
            inv = jnp.where(lane == ord_ref[b], b, inv)
        inv_vec[...] = inv
        cp = pltpu.make_async_copy(inv_vec, inv_ref, loc_sem.at[6])
        cp.start()
        return cp

    def stack_heads():
        for cp in loads:
            cp.wait()
        for a in range(2):
            for h in range(HEADS):
                src = (pl.ds(a * STRETCH, STRETCH), pl.ds(h * DIM, DIM))
                q_s[a, pl.ds(h * STRETCH, STRETCH), :] = q_in[src]
                g_s[a, pl.ds(h * STRETCH, STRETCH), :] = g_in[src]

    wait_k, wait_v = [], []
    for cp in own[:2]:
        cp.wait()
    k1 = first_stage(gk)
    for cp in own[2:]:
        cp.wait()
    v1 = first_stage(gv)
    inv_copy = invert_order()
    stack_heads()
    wait_k += k1[2]
    wait_v += v1[2]
    k2 = second_stage(gk, k1[0], k1[1], wait_k)
    v2 = second_stage(gv, v1[0], v1[1], wait_v)
    third_stage(gk, k2, wait_k)
    inv_copy.wait()

    spots, base = [], []
    for a in range(2):
        p = ord_ref[2 * me + a]
        spots.append(p)
        base.append(jnp.maximum(lax.div(p, 2) * 2 - 32, 0))

    scale = DIM ** -0.5
    log2e = 1.4426950408889634
    starts = [jnp.int32(0)]
    for d in range(3):
        starts.append(starts[-1] + len_ref[d])
    row_in = jnp.where(lane[:1] >= STRETCH, lane[:1] - STRETCH, lane[:1])
    pos_row, first_row = [], []
    for a in range(2):
        pr = spots[a] * STRETCH + row_in
        fr = jnp.zeros_like(pr)
        for st in starts:
            fr = jnp.maximum(fr, jnp.where(st <= pr, st, 0))
        pos_row.append(pr)
        first_row.append(fr)

    def window(src, dst):
        def step(w, carry):
            rows = pl.ds(pl.multiple_of(w * STRETCH, STRETCH), STRETCH)
            for a in range(2):
                dst[a, rows, :] = src[inv_ref[0, base[a] + w]]
            return carry

        lax.fori_loop(0, WIN, step, 0)

    for ref, k in wait_k:
        arrive(ref, k)
    window(gk, ksw)

    def score_step(j, carry):
        new = []
        for a in range(2):
            s = dot_nt(ksw[a, pl.ds(pl.multiple_of(j * KC, 16), KC), :], q_s[a])
            first_key = base[a] * STRETCH + j * KC
            kpos = first_key + lax.broadcasted_iota(jnp.int32, (KC, 128), 0)
            ok = (kpos <= pos_row[a]) & (kpos >= first_row[a])
            for g in range(GROUPS):
                cols = pl.ds(g * 128, 128)
                sg = jnp.where(ok, s[:, g * 128:(g + 1) * 128] * (scale * log2e), NEG)
                sbuf[a, pl.ds(pl.multiple_of(j * KC, 8), KC), cols] = sg
                new.append(jnp.maximum(carry[a * GROUPS + g], fold8(sg, jnp.max)))
        return tuple(new)

    tops = tuple(jnp.full((8, 128), NEG, F32) for _ in range(2 * GROUPS))
    tops = lax.fori_loop(0, WROWS // KC, score_step, tops)
    tops = [jnp.max(t, axis=0, keepdims=True) for t in tops]

    third_stage(gv, v2, wait_v)

    def weight_step(j, carry):
        new = []
        rows = pl.ds(pl.multiple_of(j * KC, 16), KC)
        for a in range(2):
            for g in range(GROUPS):
                cols = pl.ds(g * 128, 128)
                pw = jnp.exp2(sbuf[a, rows, cols] - tops[a * GROUPS + g])
                pbuf[a, rows, cols] = pw.astype(BF16)
                new.append(carry[a * GROUPS + g] + fold8(pw, jnp.sum))
        return tuple(new)

    zero = jnp.zeros((8, 128), F32)
    sums = tuple(zero for _ in range(2 * GROUPS))
    sums = lax.fori_loop(0, WROWS // KC, weight_step, sums)
    inv_l = [1.0 / jnp.sum(total, axis=0, keepdims=True) for total in sums]

    for a in range(2):
        for g in range(GROUPS):
            rows = pl.ds(g * 128, 128)
            col = jnp.broadcast_to(inv_l[a * GROUPS + g], (128, 128)).T
            qn_s[a, rows, :] = (q_s[a, rows, :].astype(F32) * (col * scale)).astype(BF16)
            gn_s[a, rows, :] = (g_s[a, rows, :].astype(F32) * col).astype(BF16)

    spans_of = KC // STRETCH

    def values_step(j, carry):
        rows = pl.ds(pl.multiple_of(j * KC, 16), KC)
        for a in range(2):
            dvw[a, pl.ds(j * spans_of, spans_of)] = dot_nn(pbuf[a, rows, :], gn_s[a]).reshape(spans_of, STRETCH, DIM)
        return carry

    lax.fori_loop(0, WROWS // KC, values_step, 0)
    for a in range(2):
        dkw[a, WIN] = jnp.zeros((STRETCH, DIM), F32)
        dvw[a, WIN] = jnp.zeros((STRETCH, DIM), F32)

    def rs_copy(src, dst, k, to):
        return pltpu.make_async_remote_copy(
            src_ref=src, dst_ref=dst, send_sem=rs_send.at[k], recv_sem=rs_recv.at[k],
            device_id=to, device_id_type=MESH,
        )

    def unsort(w, part, cc, k):
        def step(j, carry):
            chip = wrap(y + 2 + k) * RING + wrap(x + 2 + j)
            for half in range(2):
                s = ord_ref[2 * (2 * chip + cc) + half]
                at = []
                for a in range(2):
                    off = s - base[a]
                    at.append(jnp.where((off >= 0) & (off < WIN), off, WIN))
                part[cc, k, j, half] = (w[0, at[0]] + w[1, at[1]]).astype(BF16)
            return carry

        lax.fori_loop(0, RING, step, 0)

    def swap_start(w, part, pair, k0):
        cps = []
        for k in range(RING):
            unsort(w, part, oc, k)
            cp = rs_copy(part.at[oc, k], pair.at[k], k0 + k, sib)
            cp.start()
            cps.append(cp)
        for k in range(RING):
            unsort(w, part, c, k)
        return cps

    def scatter(part, pair, total, got, cps, k0):
        out = []
        for k in range(RING):
            cps[k].wait_recv()

            def step(j, carry):
                total[k, j] = (part[c, k, j].astype(F32) + pair[k, j].astype(F32)).astype(BF16)
                return carry

            lax.fori_loop(0, RING, step, 0)
            for j in range(RING):
                dy, dx = (2 + k) % RING, (2 + j) % RING
                if dy or dx:
                    cp = rs_copy(total.at[k, j], got.at[k, j], k0 + k * RING + j, dev(ys[dy], xs[dx], c))
                    cp.start()
                    out.append(cp)
        return out

    def collect(total, got, cps, out):
        for cp in cps:
            cp.wait_recv()
        for half in range(2):
            acc = total[2, 2, half].astype(F32)
            for k in range(RING):
                for j in range(RING):
                    if (k, j) != (2, 2):
                        acc = acc + got[k, j, half].astype(F32)
            out[pl.ds(half * STRETCH, STRETCH), :] = acc.astype(BF16)

    rs, swap_v, swap_k = [], [], []
    swap_v = swap_start(dvw, part_v, pair_v, 0)

    for ref, k in wait_v:
        arrive(ref, k)
    window(gv, vsw)

    def value_step(j, carry):
        new = []
        rows = pl.ds(pl.multiple_of(j * KC, 16), KC)
        for a in range(2):
            dp = dot_nt(vsw[a, rows, :], g_s[a])
            for g in range(GROUPS):
                cols = pl.ds(g * 128, 128)
                dpg = dp[:, g * 128:(g + 1) * 128]
                sbuf[a, rows, cols] = dpg
                new.append(carry[a * GROUPS + g] + fold8(pbuf[a, rows, cols].astype(F32) * dpg, jnp.sum))
        return tuple(new)

    sums = tuple(zero for _ in range(2 * GROUPS))
    sums = lax.fori_loop(0, WROWS // KC, value_step, sums)
    delta = [jnp.sum(t, axis=0, keepdims=True) * r for t, r in zip(sums, inv_l)]

    rs_v = []
    rs_v = scatter(part_v, pair_v, sum_v, got_v, swap_v, 8)

    def grad_step(j, carry):
        rows = pl.ds(pl.multiple_of(j * KC, 16), KC)
        for a in range(2):
            for g in range(GROUPS):
                cols = pl.ds(g * 128, 128)
                pw = pbuf[a, rows, cols].astype(F32)
                dsbuf[a, rows, cols] = (pw * (sbuf[a, rows, cols] - delta[a * GROUPS + g])).astype(BF16)
            dkw[a, pl.ds(j * spans_of, spans_of)] = dot_nn(dsbuf[a, rows, :], qn_s[a]).reshape(spans_of, STRETCH, DIM)
        return carry

    lax.fori_loop(0, WROWS // KC, grad_step, 0)

    swap_k = swap_start(dkw, part_k, pair_k, 4)
    rs_k = []
    rs_k = scatter(part_k, pair_k, sum_k, got_k, swap_k, 24)

    def turn_step(j, carry):
        rows = pl.ds(pl.multiple_of(j * 128, 128), 128)
        for a in range(2):
            ktw[a, :, rows] = ksw[a, rows, :].T
        return carry

    lax.fori_loop(0, WIN // 2, turn_step, 0)
    for a in range(2):
        dqt = dot_nn(ktw[a], dsbuf[a])
        for g in range(GROUPS):
            out = (dqt[:, g * 128:(g + 1) * 128] * (inv_l[a * GROUPS + g] * scale)).T.astype(BF16)
            for i in range(2):
                dq_ref[pl.ds(a * STRETCH, STRETCH), pl.ds((2 * g + i) * DIM, DIM)] = out[i * STRETCH:(i + 1) * STRETCH]

    collect(sum_v, got_v, rs_v, dv_ref)
    collect(sum_k, got_k, rs_k, dk_ref)
    for cp in sent + swap_v + swap_k + rs_v + rs_k:
        cp.wait_send()


def copy_out(*refs):
    for src, dst in zip(refs[:3], refs[3:]):
        dst[...] = src[...]


def body(queries, keys, values, grad_out, doc_lengths, stretch_order):
    anyspec = pl.BlockSpec(memory_space=pl.ANY)
    smem = pl.BlockSpec(memory_space=pltpu.SMEM)
    vmem = pl.BlockSpec(memory_space=pltpu.VMEM)
    half = (STRETCH, DIM)
    outs = tuple(jax.ShapeDtypeStruct(s.shape, BF16) for s in (queries, keys, values))
    grads = pl.pallas_call(
        kernel,
        out_shape=outs,
        in_specs=[anyspec] * 4 + [smem] * 2,
        out_specs=(vmem, vmem, vmem),
        scratch_shapes=[
            pltpu.VMEM((STRETCHES,) + half, BF16),
            pltpu.VMEM((STRETCHES,) + half, BF16),
            pltpu.VMEM((2 * STRETCH, HEADS * DIM), BF16),
            pltpu.VMEM((2 * STRETCH, HEADS * DIM), BF16),
            pltpu.VMEM((2, COLS, DIM), BF16),
            pltpu.VMEM((2, COLS, DIM), BF16),
            pltpu.VMEM((2, COLS, DIM), BF16),
            pltpu.VMEM((2, COLS, DIM), BF16),
            pltpu.VMEM((2, WROWS, DIM), BF16),
            pltpu.VMEM((2, WROWS, DIM), BF16),
            pltpu.VMEM((2, DIM, WROWS), BF16),
            pltpu.VMEM((2, WROWS, COLS), F32),
            pltpu.VMEM((2, WROWS, COLS), BF16),
            pltpu.VMEM((2, WROWS, COLS), BF16),
            pltpu.VMEM((2, WIN + 1) + half, F32),
            pltpu.VMEM((2, WIN + 1) + half, F32),
            pltpu.VMEM((2, RING, RING, 2) + half, BF16),
            pltpu.VMEM((2, RING, RING, 2) + half, BF16),
            pltpu.VMEM((RING, RING, 2) + half, BF16),
            pltpu.VMEM((RING, RING, 2) + half, BF16),
            pltpu.VMEM((RING, RING, 2) + half, BF16),
            pltpu.VMEM((RING, RING, 2) + half, BF16),
            pltpu.VMEM((RING, RING, 2) + half, BF16),
            pltpu.VMEM((RING, RING, 2) + half, BF16),
            pltpu.VMEM((8, 128), jnp.int32),
            pltpu.SMEM((8, 128), jnp.int32),
            pltpu.SemaphoreType.DMA((7,)),
            pltpu.SemaphoreType.DMA((N_AG,)),
            pltpu.SemaphoreType.DMA((N_AG,)),
            pltpu.SemaphoreType.DMA((N_RS,)),
            pltpu.SemaphoreType.DMA((N_RS,)),
        ],
        compiler_params=pltpu.CompilerParams(
            collective_id=0, has_side_effects=True, vmem_limit_bytes=58 * 1024 * 1024
        ),
    )(queries, keys, values, grad_out, doc_lengths, stretch_order)
    return pl.pallas_call(
        copy_out,
        out_shape=outs,
        in_specs=[vmem] * 3,
        out_specs=(vmem,) * 3,
    )(*grads)


def solution(mesh):
    return jax.shard_map(
        body,
        mesh=mesh,
        in_specs=(P("ctx", "head"), P("ctx", "head"), P("ctx", "head"), P("ctx", "head"), P(), P()),
        out_specs=(P("ctx", "head"), P("ctx", "head"), P("ctx", "head")),
        check_vma=False,
    )
```

```python
import functools

import jax
import jax.numpy as jnp
from jax import lax
from jax.experimental import pallas as pl
from jax.experimental.pallas import tpu as pltpu
from jax.sharding import PartitionSpec as P

MESH = pl.DeviceIdType.MESH
F32, BF16 = jnp.float32, jnp.bfloat16
RING = 4
CHIPS = RING * RING
HEADS, DIM = 8, 128
STRETCH = 64
STRETCHES = 64
COLS = HEADS * STRETCH
GROUPS = COLS // 128
WIN = 34
WROWS = WIN * STRETCH
KC = 1088
NEG = -1e30
N_AG = 128
N_RS = 96
HERE = 2


def dot_nt(a, b):
    return lax.dot_general(a, b, (((1,), (1,)), ((), ())), preferred_element_type=F32)


def dot_nn(a, b):
    return lax.dot_general(a, b, (((1,), (0,)), ((), ())), preferred_element_type=F32)


def fold8(v, op):
    return op(v.reshape(v.shape[0] // 8, 8, v.shape[1]), axis=0)


def kernel(
    q_hbm, k_hbm, v_hbm, g_hbm, len_ref, ord_ref,
    dq_ref, dk_ref, dv_ref,
    gk, gv, q_in, g_in, q_s, g_s, qn_s, gn_s, ksw, vsw, ktw, sbuf, pbuf, dsbuf, dkw, dvw,
    part_k, part_v, pair_k, pair_v, sum_k, sum_v, got_k, got_v, mid_k, mid_v, last_k, last_v, inv_vec, inv_ref,
    loc_sem, ag_send, ag_recv, rs_send, rs_recv,
):
    me = lax.axis_index("ctx")
    head = lax.axis_index("head")
    c = lax.rem(me, 2)
    x = lax.rem(lax.div(me, 2), RING)
    y = lax.div(me, 2 * RING)
    oc = 1 - c

    def wrap(v):
        return lax.rem(v, RING)

    xs = [wrap(x + d) for d in range(RING)]
    ys = [wrap(y + d) for d in range(RING)]
    x2, y2 = xs[2], ys[2]

    def dev(yy, xx, cc):
        return ((yy * RING + xx) * 2 + cc, head)

    sib = dev(y, x, oc)

    own = []
    for i, (src, dst) in enumerate(((k_hbm, gk), (v_hbm, gv))):
        for h in range(2):
            rows = pl.ds(h * STRETCH, STRETCH)
            own.append(pltpu.make_async_copy(src.at[rows], dst.at[2 * me + h], loc_sem.at[2 * i + h]))
    loads = [
        pltpu.make_async_copy(q_hbm, q_in, loc_sem.at[4]),
        pltpu.make_async_copy(g_hbm, g_in, loc_sem.at[5]),
    ]
    for cp in own + loads:
        cp.start()

    barrier = pltpu.get_barrier_semaphore()
    peers = [dev(y, xs[d], c) for d in (1, 2, 3)] + [dev(ys[d], x, c) for d in (1, 2, 3)] + [sib]
    for peer in peers:
        pl.semaphore_signal(barrier, inc=1, device_id=peer, device_id_type=MESH)
    pl.semaphore_wait(barrier, len(peers))

    sent = []
    count = [0]

    def send(ref, to):
        k = count[0]
        count[0] += 1
        cp = pltpu.make_async_remote_copy(
            src_ref=ref, dst_ref=ref, send_sem=ag_send.at[k], recv_sem=ag_recv.at[k],
            device_id=to, device_id_type=MESH,
        )
        cp.start()
        sent.append(cp)
        return k

    def arrive(ref, k):
        pltpu.make_async_remote_copy(
            src_ref=ref, dst_ref=ref, send_sem=ag_send.at[k], recv_sem=ag_recv.at[k],
            device_id=sib, device_id_type=MESH,
        ).wait_recv()

    def block(yy, xx, cc):
        return ((yy * RING + xx) * 2 + cc) * 2

    def node(buf, yy, xx, cc):
        return buf.at[pl.ds(block(yy, xx, cc), 2)]

    def part_of(buf, yy, xx, cc, half):
        return buf.at[block(yy, xx, cc) + half]

    far_first, near_first, group_order = (2, 1, 3), (1, 3, 2), (0, 1, 3, 2)

    def first_stage(buf):
        mine = node(buf, y, x, c)
        along_x = {d: send(mine, dev(y, xs[d], c)) for d in far_first}
        along_y = {d: send(mine, dev(ys[d], x, c)) for d in far_first}
        return along_x, along_y, [(node(buf, y, x, oc), send(mine, sib))]

    def second_stage(buf, along_x, along_y, pending):
        coming = []
        for d in near_first:
            xx, yy = xs[RING - d], ys[RING - d]
            arrive(node(buf, y, xx, c), along_x[d])
            k = send(part_of(buf, y, xx, c, 0), dev(ys[2], x, c))
            coming.append((2, y2, xx, 0, k))
            arrive(node(buf, yy, x, c), along_y[d])
            k = send(part_of(buf, yy, x, c, 1), dev(y, xs[2], c))
            coming.append((2, yy, x2, 1, k))
        for d in near_first:
            xx, yy = xs[RING - d], ys[RING - d]
            for e in (1, 3):
                k = send(part_of(buf, y, xx, c, 0), dev(ys[e], x, c))
                coming.append((e, ys[RING - e], xx, 0, k))
                k = send(part_of(buf, yy, x, c, 1), dev(y, xs[e], c))
                coming.append((e, yy, xs[RING - e], 1, k))
        for d in near_first:
            xx, yy = xs[RING - d], ys[RING - d]
            pending.append((node(buf, y, xx, oc), send(node(buf, y, xx, c), sib)))
            pending.append((node(buf, yy, x, oc), send(node(buf, yy, x, c), sib)))
        return coming

    def third_stage(buf, coming, pending):
        for e in far_first:
            for ee, yy, xx, half, k in coming:
                if ee == e:
                    arrive(part_of(buf, yy, xx, c, half), k)
                    pending.append((part_of(buf, yy, xx, oc, half), send(part_of(buf, yy, xx, c, half), sib)))

    lane = lax.broadcasted_iota(jnp.int32, (8, 128), 1)

    def invert_order():
        inv = jnp.zeros((8, 128), jnp.int32)
        for b in range(STRETCHES):
            inv = jnp.where(lane == ord_ref[b], b, inv)
        inv_vec[...] = inv
        cp = pltpu.make_async_copy(inv_vec, inv_ref, loc_sem.at[6])
        cp.start()
        return cp

    def stack_heads():
        for cp in loads:
            cp.wait()
        for a in range(2):
            for h in range(HEADS):
                src = (pl.ds(a * STRETCH, STRETCH), pl.ds(h * DIM, DIM))
                q_s[a, pl.ds(h * STRETCH, STRETCH), :] = q_in[src]
                g_s[a, pl.ds(h * STRETCH, STRETCH), :] = g_in[src]

    wait_k, wait_v = [], []
    for cp in own[:2]:
        cp.wait()
    k1 = first_stage(gk)
    for cp in own[2:]:
        cp.wait()
    v1 = first_stage(gv)
    inv_copy = invert_order()
    wait_k += k1[2]
    wait_v += v1[2]
    k2 = second_stage(gk, k1[0], k1[1], wait_k)
    v2 = second_stage(gv, v1[0], v1[1], wait_v)
    stack_heads()
    third_stage(gk, k2, wait_k)
    inv_copy.wait()

    spots, base = [], []
    for a in range(2):
        p = ord_ref[2 * me + a]
        spots.append(p)
        base.append(jnp.maximum(lax.div(p, 2) * 2 - 32, 0))

    scale = DIM ** -0.5
    log2e = 1.4426950408889634
    starts = [jnp.int32(0)]
    for d in range(3):
        starts.append(starts[-1] + len_ref[d])
    row_in = jnp.where(lane[:1] >= STRETCH, lane[:1] - STRETCH, lane[:1])
    pos_row, first_row = [], []
    for a in range(2):
        pr = spots[a] * STRETCH + row_in
        fr = jnp.zeros_like(pr)
        for st in starts:
            fr = jnp.maximum(fr, jnp.where(st <= pr, st, 0))
        pos_row.append(pr)
        first_row.append(fr)

    def window(src, dst):
        def step(w, carry):
            rows = pl.ds(pl.multiple_of(w * STRETCH, STRETCH), STRETCH)
            for a in range(2):
                dst[a, rows, :] = src[inv_ref[0, base[a] + w]]
            return carry

        lax.fori_loop(0, WIN, step, 0, unroll=17)

    for ref, k in wait_k:
        arrive(ref, k)
    window(gk, ksw)

    def score_step(j, carry):
        new = []
        for a in range(2):
            s = dot_nt(ksw[a, pl.ds(pl.multiple_of(j * KC, 16), KC), :], q_s[a])
            first_key = base[a] * STRETCH + j * KC
            kpos = first_key + lax.broadcasted_iota(jnp.int32, (KC, 128), 0)
            ok = (kpos <= pos_row[a]) & (kpos >= first_row[a])
            for g in range(GROUPS):
                cols = pl.ds(g * 128, 128)
                sg = jnp.where(ok, s[:, g * 128:(g + 1) * 128] * (scale * log2e), NEG)
                sbuf[a, pl.ds(pl.multiple_of(j * KC, 8), KC), cols] = sg
                new.append(jnp.maximum(carry[a * GROUPS + g], fold8(sg, jnp.max)))
        return tuple(new)

    tops = tuple(jnp.full((8, 128), NEG, F32) for _ in range(2 * GROUPS))
    tops = lax.fori_loop(0, WROWS // KC, score_step, tops)
    tops = [jnp.max(t, axis=0, keepdims=True) for t in tops]

    def weight_step(j, carry):
        new = []
        rows = pl.ds(pl.multiple_of(j * KC, 16), KC)
        for a in range(2):
            for g in range(GROUPS):
                cols = pl.ds(g * 128, 128)
                pw = jnp.exp2(sbuf[a, rows, cols] - tops[a * GROUPS + g])
                pbuf[a, rows, cols] = pw.astype(BF16)
                new.append(carry[a * GROUPS + g] + fold8(pw, jnp.sum))
        return tuple(new)

    zero = jnp.zeros((8, 128), F32)
    sums = tuple(zero for _ in range(2 * GROUPS))
    sums = lax.fori_loop(0, WROWS // KC, weight_step, sums)
    third_stage(gv, v2, wait_v)
    inv_l = [1.0 / jnp.sum(total, axis=0, keepdims=True) for total in sums]

    for a in range(2):
        for g in range(GROUPS):
            rows = pl.ds(g * 128, 128)
            col = jnp.broadcast_to(inv_l[a * GROUPS + g], (128, 128)).T
            qn_s[a, rows, :] = (q_s[a, rows, :].astype(F32) * (col * scale)).astype(BF16)
            gn_s[a, rows, :] = (g_s[a, rows, :].astype(F32) * col).astype(BF16)

    spans_of = KC // STRETCH

    for a in range(2):
        dkw[a, WIN] = jnp.zeros((STRETCH, DIM), F32)
        dvw[a, WIN] = jnp.zeros((STRETCH, DIM), F32)

    def rs_copy(src, dst, k, to):
        return pltpu.make_async_remote_copy(
            src_ref=src, dst_ref=dst, send_sem=rs_send.at[k], recv_sem=rs_recv.at[k],
            device_id=to, device_id_type=MESH,
        )

    def unsort(w, part, cc, i):
        def step(g, carry):
            for half in range(2):
                dy, dx = (i, g) if half == 0 else (g, i)
                chip = wrap(y + 2 + dy) * RING + wrap(x + 2 + dx)
                s = ord_ref[2 * (2 * chip + cc) + half]
                at = []
                for a in range(2):
                    off = s - base[a]
                    at.append(jnp.where((off >= 0) & (off < WIN), off, WIN))
                part[cc, i, half, g] = (w[0, at[0]] + w[1, at[1]]).astype(BF16)
            return carry

        lax.fori_loop(0, RING, step, 0, unroll=True)

    def swap_start(w, part, pair, k0):
        cps = {}
        for i in group_order:
            unsort(w, part, oc, i)
            cps[i] = rs_copy(part.at[oc, i], pair.at[i], k0 + i, sib)
            cps[i].start()
        return cps

    def ring_peer(half, g):
        return dev(y, xs[(2 + g) % RING], c) if half == 0 else dev(ys[(2 + g) % RING], x, c)

    def scatter_rings(w, part, pair, total, got, cps, k0):
        out = {}
        for i in group_order:
            unsort(w, part, c, i)
            cps[i].wait_recv()
            for g in group_order:
                for half in range(2):
                    both = part[c, i, half, g].astype(F32) + pair[i, half, g].astype(F32)
                    total[i, half, g] = both.astype(BF16)
                    if g != HERE:
                        k = k0 + (i * 2 + half) * RING + g
                        cp = rs_copy(total.at[i, half, g], got.at[i, half, g], k, ring_peer(half, g))
                        cp.start()
                        out[i, half, g] = cp
        return out

    def scatter_rest(total, got, mid, last, cps, k0):
        out = []
        for i in group_order:
            for half in range(2):
                acc = total[i, half, HERE].astype(F32)
                for g in group_order[:3]:
                    cps[i, half, g].wait_recv()
                    acc = acc + got[i, half, g].astype(F32)
                mid[half, i] = acc.astype(BF16)
                if i != HERE:
                    cp = rs_copy(mid.at[half, i], last.at[half, i], k0 + 2 * i + half, ring_peer(1 - half, i))
                    cp.start()
                    out.append(cp)
        return out

    def collect_rest(mid, last, cps, out):
        for cp in cps:
            cp.wait_recv()
        for half in range(2):
            acc = mid[half, HERE].astype(F32)
            for i in group_order[:3]:
                acc = acc + last[half, i].astype(F32)
            out[pl.ds(half * STRETCH, STRETCH), :] = acc.astype(BF16)

    swap_v, swap_k, rs_v, rs_v2, rs_k, rs_k2 = {}, {}, {}, [], {}, []
    def values_step(j, carry):
        rows = pl.ds(pl.multiple_of(j * KC, 16), KC)
        for a in range(2):
            dvw[a, pl.ds(j * spans_of, spans_of)] = dot_nn(pbuf[a, rows, :], gn_s[a]).reshape(spans_of, STRETCH, DIM)
        return carry

    lax.fori_loop(0, WROWS // KC, values_step, 0)
    swap_v = swap_start(dvw, part_v, pair_v, 0)

    for ref, k in wait_v:
        arrive(ref, k)
    window(gv, vsw)

    def value_step(j, carry):
        new = []
        rows = pl.ds(pl.multiple_of(j * KC, 16), KC)
        for a in range(2):
            dp = dot_nt(vsw[a, rows, :], g_s[a])
            for g in range(GROUPS):
                cols = pl.ds(g * 128, 128)
                dpg = dp[:, g * 128:(g + 1) * 128]
                sbuf[a, rows, cols] = dpg
                new.append(carry[a * GROUPS + g] + fold8(pbuf[a, rows, cols].astype(F32) * dpg, jnp.sum))
        return tuple(new)

    sums = tuple(zero for _ in range(2 * GROUPS))
    sums = lax.fori_loop(0, WROWS // KC, value_step, sums)
    delta = [jnp.sum(t, axis=0, keepdims=True) * r for t, r in zip(sums, inv_l)]

    rs_v = scatter_rings(dvw, part_v, pair_v, sum_v, got_v, swap_v, 8)

    def grad_step(j, carry):
        rows = pl.ds(pl.multiple_of(j * KC, 16), KC)
        for a in range(2):
            for g in range(GROUPS):
                cols = pl.ds(g * 128, 128)
                pw = pbuf[a, rows, cols].astype(F32)
                dsbuf[a, rows, cols] = (pw * (sbuf[a, rows, cols] - delta[a * GROUPS + g])).astype(BF16)
            dkw[a, pl.ds(j * spans_of, spans_of)] = dot_nn(dsbuf[a, rows, :], qn_s[a]).reshape(spans_of, STRETCH, DIM)
        return carry

    lax.fori_loop(0, WROWS // KC, grad_step, 0)

    swap_k = swap_start(dkw, part_k, pair_k, 4)

    rs_k = scatter_rings(dkw, part_k, pair_k, sum_k, got_k, swap_k, 40)

    def turn_step(j, carry):
        rows = pl.ds(pl.multiple_of(j * 128, 128), 128)
        for a in range(2):
            ktw[a, :, rows] = ksw[a, rows, :].T
        return carry

    lax.fori_loop(0, WIN // 2, turn_step, 0)
    def queries_out():
        for a in range(2):
            dqt = dot_nn(ktw[a], dsbuf[a])
            for g in range(GROUPS):
                out = (dqt[:, g * 128:(g + 1) * 128] * (inv_l[a * GROUPS + g] * scale)).T.astype(BF16)
                for i in range(2):
                    dq_ref[pl.ds(a * STRETCH, STRETCH), pl.ds((2 * g + i) * DIM, DIM)] = out[i * STRETCH:(i + 1) * STRETCH]

    rs_v2 = scatter_rest(sum_v, got_v, mid_v, last_v, rs_v, 72)
    queries_out()
    rs_k2 = scatter_rest(sum_k, got_k, mid_k, last_k, rs_k, 80)
    collect_rest(mid_v, last_v, rs_v2, dv_ref)
    collect_rest(mid_k, last_k, rs_k2, dk_ref)
    grouped = [cp for group in (swap_v, swap_k, rs_v, rs_k) for cp in group.values()]
    for cp in sent + grouped + rs_v2 + rs_k2:
        cp.wait_send()


def copy_out(*refs):
    sem = refs[6]
    cps = [pltpu.make_async_copy(refs[i], refs[i + 3], sem.at[i]) for i in range(3)]
    for cp in cps:
        cp.start()
    for cp in cps:
        cp.wait()


def body(queries, keys, values, grad_out, doc_lengths, stretch_order):
    anyspec = pl.BlockSpec(memory_space=pl.ANY)
    smem = pl.BlockSpec(memory_space=pltpu.SMEM)
    vmem = pl.BlockSpec(memory_space=pltpu.VMEM)
    half = (STRETCH, DIM)
    outs = tuple(jax.ShapeDtypeStruct(s.shape, BF16) for s in (queries, keys, values))
    kept = tuple(pltpu.VMEM(s.shape, BF16) for s in outs)
    hbm = pl.BlockSpec(memory_space=pltpu.HBM)
    grads = pl.pallas_call(
        kernel,
        out_shape=kept,
        in_specs=[hbm] * 4 + [smem] * 2,
        out_specs=(vmem, vmem, vmem),
        scratch_shapes=[
            pltpu.VMEM((STRETCHES,) + half, BF16),
            pltpu.VMEM((STRETCHES,) + half, BF16),
            pltpu.VMEM((2 * STRETCH, HEADS * DIM), BF16),
            pltpu.VMEM((2 * STRETCH, HEADS * DIM), BF16),
            pltpu.VMEM((2, COLS, DIM), BF16),
            pltpu.VMEM((2, COLS, DIM), BF16),
            pltpu.VMEM((2, COLS, DIM), BF16),
            pltpu.VMEM((2, COLS, DIM), BF16),
            pltpu.VMEM((2, WROWS, DIM), BF16),
            pltpu.VMEM((2, WROWS, DIM), BF16),
            pltpu.VMEM((2, DIM, WROWS), BF16),
            pltpu.VMEM((2, WROWS, COLS), F32),
            pltpu.VMEM((2, WROWS, COLS), BF16),
            pltpu.VMEM((2, WROWS, COLS), BF16),
            pltpu.VMEM((2, WIN + 1) + half, F32),
            pltpu.VMEM((2, WIN + 1) + half, F32),
            pltpu.VMEM((2, RING, 2, RING) + half, BF16),
            pltpu.VMEM((2, RING, 2, RING) + half, BF16),
            pltpu.VMEM((RING, 2, RING) + half, BF16),
            pltpu.VMEM((RING, 2, RING) + half, BF16),
            pltpu.VMEM((RING, 2, RING) + half, BF16),
            pltpu.VMEM((RING, 2, RING) + half, BF16),
            pltpu.VMEM((RING, 2, RING) + half, BF16),
            pltpu.VMEM((RING, 2, RING) + half, BF16),
            pltpu.VMEM((2, RING) + half, BF16),
            pltpu.VMEM((2, RING) + half, BF16),
            pltpu.VMEM((2, RING) + half, BF16),
            pltpu.VMEM((2, RING) + half, BF16),
            pltpu.VMEM((8, 128), jnp.int32),
            pltpu.SMEM((8, 128), jnp.int32),
            pltpu.SemaphoreType.DMA((7,)),
            pltpu.SemaphoreType.DMA((N_AG,)),
            pltpu.SemaphoreType.DMA((N_AG,)),
            pltpu.SemaphoreType.DMA((N_RS,)),
            pltpu.SemaphoreType.DMA((N_RS,)),
        ],
        compiler_params=pltpu.CompilerParams(
            collective_id=0, has_side_effects=True, vmem_limit_bytes=58 * 1024 * 1024
        ),
    )(queries, keys, values, grad_out, doc_lengths, stretch_order)
    return pl.pallas_call(
        copy_out,
        out_shape=outs,
        in_specs=[vmem] * 3,
        out_specs=(hbm,) * 3,
        scratch_shapes=[pltpu.SemaphoreType.DMA((3,))],
    )(*(pltpu.with_memory_space_constraint(t, pltpu.VMEM) for t in grads))


def solution(mesh):
    return jax.shard_map(
        body,
        mesh=mesh,
        in_specs=(P("ctx", "head"), P("ctx", "head"), P("ctx", "head"), P("ctx", "head"), P(), P()),
        out_specs=(P("ctx", "head"), P("ctx", "head"), P("ctx", "head")),
        check_vma=False,
    )
```

```python
import functools

import jax
import jax.numpy as jnp
from jax import lax
from jax.experimental import pallas as pl
from jax.experimental.pallas import tpu as pltpu
from jax.sharding import PartitionSpec as P

MESH = pl.DeviceIdType.MESH
F32, BF16 = jnp.float32, jnp.bfloat16
RING = 4
CHIPS = RING * RING
HEADS, DIM = 8, 128
STRETCH = 64
STRETCHES = 64
COLS = HEADS * STRETCH
GROUPS = COLS // 128
WIN = 34
WROWS = WIN * STRETCH
KC = 1088
ROWS = 128
BLOCKS = WROWS // ROWS
NEG = -1e30
N_AG = 128
N_RS = 96
HERE = 2


def dot_nt(a, b):
    return lax.dot_general(a, b, (((1,), (1,)), ((), ())), preferred_element_type=F32)


def dot_nn(a, b):
    return lax.dot_general(a, b, (((1,), (0,)), ((), ())), preferred_element_type=F32)


def fold8(v, op):
    return op(v.reshape(v.shape[0] // 8, 8, v.shape[1]), axis=0)


def kernel(
    q_hbm, k_hbm, v_hbm, g_hbm, len_ref, ord_ref,
    dq_ref, dk_ref, dv_ref,
    gk, gv, q_in, g_in, q_s, g_s, qn_s, gn_s, ksw, vsw, ktw, sbuf, pbuf, dsbuf, dkw, dvw,
    part_k, part_v, pair_k, pair_v, sum_k, sum_v, got_k, got_v, mid_k, mid_v, last_k, last_v, inv_vec, inv_ref,
    loc_sem, ag_send, ag_recv, rs_send, rs_recv,
):
    me = lax.axis_index("ctx")
    head = lax.axis_index("head")
    c = lax.rem(me, 2)
    x = lax.rem(lax.div(me, 2), RING)
    y = lax.div(me, 2 * RING)
    oc = 1 - c

    def wrap(v):
        return lax.rem(v, RING)

    xs = [wrap(x + d) for d in range(RING)]
    ys = [wrap(y + d) for d in range(RING)]
    x2, y2 = xs[2], ys[2]

    def dev(yy, xx, cc):
        return ((yy * RING + xx) * 2 + cc, head)

    sib = dev(y, x, oc)

    barrier = pltpu.get_barrier_semaphore()
    peers = [dev(y, xs[d], c) for d in (1, 2, 3)] + [dev(ys[d], x, c) for d in (1, 2, 3)] + [sib]
    for peer in peers:
        pl.semaphore_signal(barrier, inc=1, device_id=peer, device_id_type=MESH)
    own = []
    for i, (src, dst) in enumerate(((k_hbm, gk), (v_hbm, gv))):
        for h in range(2):
            rows = pl.ds(h * STRETCH, STRETCH)
            own.append(pltpu.make_async_copy(src.at[rows], dst.at[2 * me + h], loc_sem.at[2 * i + h]))
    loads = [
        pltpu.make_async_copy(q_hbm, q_in, loc_sem.at[4]),
        pltpu.make_async_copy(g_hbm, g_in, loc_sem.at[5]),
    ]
    for cp in own + loads:
        cp.start()

    pl.semaphore_wait(barrier, len(peers))

    sent = []
    count = [0]

    def send(ref, to):
        k = count[0]
        count[0] += 1
        cp = pltpu.make_async_remote_copy(
            src_ref=ref, dst_ref=ref, send_sem=ag_send.at[k], recv_sem=ag_recv.at[k],
            device_id=to, device_id_type=MESH,
        )
        cp.start()
        sent.append(cp)
        return k

    def arrive(ref, k):
        pltpu.make_async_remote_copy(
            src_ref=ref, dst_ref=ref, send_sem=ag_send.at[k], recv_sem=ag_recv.at[k],
            device_id=sib, device_id_type=MESH,
        ).wait_recv()

    def block(yy, xx, cc):
        return ((yy * RING + xx) * 2 + cc) * 2

    def node(buf, yy, xx, cc):
        return buf.at[pl.ds(block(yy, xx, cc), 2)]

    def part_of(buf, yy, xx, cc, half):
        return buf.at[block(yy, xx, cc) + half]

    far_first, near_first, group_order = (2, 1, 3), (1, 3, 2), (0, 1, 3, 2)

    def first_halves(buf):
        along_x = {d: send(part_of(buf, y, x, c, 0), dev(y, xs[d], c)) for d in far_first}
        along_y = {d: send(part_of(buf, y, x, c, 1), dev(ys[d], x, c)) for d in far_first}
        return along_x, along_y

    def other_halves(buf, pending):
        along_x = {d: send(part_of(buf, y, x, c, 1), dev(y, xs[d], c)) for d in far_first}
        along_y = {d: send(part_of(buf, y, x, c, 0), dev(ys[d], x, c)) for d in far_first}
        pending.append((node(buf, y, x, oc), send(node(buf, y, x, c), sib)))
        return along_x, along_y

    def second_stage(buf, along_x, along_y):
        coming = []
        for d in near_first:
            xx, yy = xs[RING - d], ys[RING - d]
            arrive(part_of(buf, y, xx, c, 0), along_x[d])
            for e in far_first:
                k = send(part_of(buf, y, xx, c, 0), dev(ys[e], x, c))
                coming.append((e, ys[RING - e], xx, 0, k))
            arrive(part_of(buf, yy, x, c, 1), along_y[d])
            for e in far_first:
                k = send(part_of(buf, yy, x, c, 1), dev(y, xs[e], c))
                coming.append((e, yy, xs[RING - e], 1, k))
        return coming

    def share_first(buf, along_x, along_y, pending):
        for d in near_first:
            xx, yy = xs[RING - d], ys[RING - d]
            arrive(part_of(buf, y, xx, c, 1), along_x[d])
            pending.append((node(buf, y, xx, oc), send(node(buf, y, xx, c), sib)))
            arrive(part_of(buf, yy, x, c, 0), along_y[d])
            pending.append((node(buf, yy, x, oc), send(node(buf, yy, x, c), sib)))

    def share_second(buf, coming, pending, which):
        for e in which:
            for ee, yy, xx, half, k in coming:
                if ee == e:
                    arrive(part_of(buf, yy, xx, c, half), k)
                    pending.append((part_of(buf, yy, xx, oc, half), send(part_of(buf, yy, xx, c, half), sib)))

    lane = lax.broadcasted_iota(jnp.int32, (8, 128), 1)

    def invert_order():
        inv = jnp.zeros((8, 128), jnp.int32)
        for b in range(STRETCHES):
            inv = jnp.where(lane == ord_ref[b], b, inv)
        inv_vec[...] = inv
        cp = pltpu.make_async_copy(inv_vec, inv_ref, loc_sem.at[6])
        cp.start()
        return cp

    def stack_heads():
        for cp in loads:
            cp.wait()
        for a in range(2):
            for h in range(HEADS):
                src = (pl.ds(a * STRETCH, STRETCH), pl.ds(h * DIM, DIM))
                q_s[a, pl.ds(h * STRETCH, STRETCH), :] = q_in[src]
                g_s[a, pl.ds(h * STRETCH, STRETCH), :] = g_in[src]

    wait_k, wait_v = [], []
    for cp in own[:2]:
        cp.wait()
    k1 = first_halves(gk)
    for cp in own[2:]:
        cp.wait()
    v1 = first_halves(gv)
    k1b = other_halves(gk, wait_k)
    v1b = other_halves(gv, wait_v)
    inv_copy = invert_order()
    k2 = second_stage(gk, *k1)
    v2 = second_stage(gv, *v1)
    share_first(gk, *k1b, wait_k)
    stack_heads()
    share_second(gk, k2, wait_k, near_first)
    share_first(gv, *v1b, wait_v)
    inv_copy.wait()

    spots, base = [], []
    for a in range(2):
        p = ord_ref[2 * me + a]
        spots.append(p)
        base.append(jnp.maximum(lax.div(p, 2) * 2 - 32, 0))

    scale = DIM ** -0.5
    log2e = 1.4426950408889634
    starts = [jnp.int32(0)]
    for d in range(3):
        starts.append(starts[-1] + len_ref[d])
    row_in = jnp.where(lane[:1] >= STRETCH, lane[:1] - STRETCH, lane[:1])
    pos_row, first_row = [], []
    for a in range(2):
        pr = spots[a] * STRETCH + row_in
        fr = jnp.zeros_like(pr)
        for st in starts:
            fr = jnp.maximum(fr, jnp.where(st <= pr, st, 0))
        pos_row.append(pr)
        first_row.append(fr)

    def window(src, dst):
        def step(w, carry):
            rows = pl.ds(pl.multiple_of(w * STRETCH, STRETCH), STRETCH)
            for a in range(2):
                dst[a, rows, :] = src[inv_ref[0, base[a] + w]]
            return carry

        lax.fori_loop(0, WIN, step, 0, unroll=17)

    for ref, k in wait_k:
        arrive(ref, k)
    window(gk, ksw)

    def key_rows(i):
        return pl.ds(i * ROWS, ROWS)

    def scores(a):
        tops = [jnp.full((8, 128), NEG, F32)] * GROUPS

        def raise_tops(i):
            for g in range(GROUPS):
                tops[g] = jnp.maximum(tops[g], fold8(sbuf[a, key_rows(i), pl.ds(g * 128, 128)], jnp.max))

        for i in range(BLOCKS):
            s = dot_nt(ksw[a, key_rows(i), :], q_s[a])
            kpos = base[a] * STRETCH + i * ROWS + lax.broadcasted_iota(jnp.int32, (ROWS, 128), 0)
            ok = (kpos <= pos_row[a]) & (kpos >= first_row[a])
            for g in range(GROUPS):
                sg = jnp.where(ok, s[:, g * 128:(g + 1) * 128] * (scale * log2e), NEG)
                sbuf[a, key_rows(i), pl.ds(g * 128, 128)] = sg
            if i:
                raise_tops(i - 1)
        raise_tops(BLOCKS - 1)
        return [jnp.max(t, axis=0, keepdims=True) for t in tops]

    def weights(a, i, sums):
        for g in range(GROUPS):
            cols = pl.ds(g * 128, 128)
            pw = jnp.exp2(sbuf[a, key_rows(i), cols] - tops[a][g])
            pbuf[a, key_rows(i), cols] = pw.astype(BF16)
            sums[g] = sums[g] + fold8(pw, jnp.sum)

    def inverse_sums(a, sums):
        for g in range(GROUPS):
            inv_l.append(1.0 / jnp.sum(sums[g], axis=0, keepdims=True))

    def column(a, g):
        return jnp.broadcast_to(inv_l[a * GROUPS + g], (128, 128)).T

    def scaled_grads(a):
        for g in range(GROUPS):
            rows = pl.ds(g * 128, 128)
            gn_s[a, rows, :] = (g_s[a, rows, :].astype(F32) * column(a, g)).astype(BF16)

    def scaled_queries():
        for a in range(2):
            for g in range(GROUPS):
                rows = pl.ds(g * 128, 128)
                qn_s[a, rows, :] = (q_s[a, rows, :].astype(F32) * (column(a, g) * scale)).astype(BF16)

    def value_grads(a, i):
        part = dot_nn(pbuf[a, key_rows(i), :], gn_s[a])
        dvw[a, pl.ds(i * (ROWS // STRETCH), ROWS // STRETCH)] = part.reshape(ROWS // STRETCH, STRETCH, DIM)

    zero = jnp.zeros((8, 128), F32)
    tops, inv_l = [], []
    for a in range(2):
        tops.append([jnp.zeros((1, 128), F32)] * GROUPS)
    tops[0] = scores(0)
    share_second(gv, v2, wait_v, near_first[:2])
    tops[1] = scores(1)
    share_second(gv, v2, wait_v, near_first[2:])
    sums = [zero] * GROUPS
    for i in range(BLOCKS):
        weights(0, i, sums)
    inverse_sums(0, sums)
    scaled_grads(0)
    sums = [zero] * GROUPS
    for i in range(BLOCKS):
        value_grads(0, i)
        weights(1, i, sums)
    inverse_sums(1, sums)
    scaled_grads(1)
    for i in range(BLOCKS):
        value_grads(1, i)

    spans_of = KC // STRETCH

    def spare_blocks():
        for a in range(2):
            dkw[a, WIN] = jnp.zeros((STRETCH, DIM), F32)
            dvw[a, WIN] = jnp.zeros((STRETCH, DIM), F32)

    spare_blocks()

    def rs_copy(src, dst, k, to):
        return pltpu.make_async_remote_copy(
            src_ref=src, dst_ref=dst, send_sem=rs_send.at[k], recv_sem=rs_recv.at[k],
            device_id=to, device_id_type=MESH,
        )

    def unsort(w, part, cc, i):
        def step(g, carry):
            for half in range(2):
                dy, dx = (i, g) if half == 0 else (g, i)
                chip = wrap(y + 2 + dy) * RING + wrap(x + 2 + dx)
                s = ord_ref[2 * (2 * chip + cc) + half]
                at = []
                for a in range(2):
                    off = s - base[a]
                    at.append(jnp.where((off >= 0) & (off < WIN), off, WIN))
                part[cc, i, half, g] = (w[0, at[0]] + w[1, at[1]]).astype(BF16)
            return carry

        lax.fori_loop(0, RING, step, 0, unroll=True)

    def swap_start(w, part, pair, k0):
        cps = {}
        for i in group_order:
            unsort(w, part, oc, i)
            cps[i] = rs_copy(part.at[oc, i], pair.at[i], k0 + i, sib)
            cps[i].start()
        return cps

    def ring_peer(half, g):
        return dev(y, xs[(2 + g) % RING], c) if half == 0 else dev(ys[(2 + g) % RING], x, c)

    def scatter_rings(w, part, pair, total, got, cps, k0):
        out = {}
        for i in group_order:
            unsort(w, part, c, i)
            cps[i].wait_recv()
            for g in group_order:
                for half in range(2):
                    both = part[c, i, half, g].astype(F32) + pair[i, half, g].astype(F32)
                    total[i, half, g] = both.astype(BF16)
                    if g != HERE:
                        k = k0 + (i * 2 + half) * RING + g
                        cp = rs_copy(total.at[i, half, g], got.at[i, half, g], k, ring_peer(half, g))
                        cp.start()
                        out[i, half, g] = cp
        return out

    def scatter_rest(total, got, mid, last, cps, k0):
        out = []
        for i in group_order:
            for half in range(2):
                acc = total[i, half, HERE].astype(F32)
                for g in group_order[:3]:
                    cps[i, half, g].wait_recv()
                    acc = acc + got[i, half, g].astype(F32)
                mid[half, i] = acc.astype(BF16)
                if i != HERE:
                    cp = rs_copy(mid.at[half, i], last.at[half, i], k0 + 2 * i + half, ring_peer(1 - half, i))
                    cp.start()
                    out.append(cp)
        return out

    def collect_rest(mid, last, cps, out):
        for cp in cps:
            cp.wait_recv()
        for half in range(2):
            acc = mid[half, HERE].astype(F32)
            for i in group_order[:3]:
                acc = acc + last[half, i].astype(F32)
            out[pl.ds(half * STRETCH, STRETCH), :] = acc.astype(BF16)

    swap_v, swap_k, rs_v, rs_v2, rs_k, rs_k2 = {}, {}, {}, [], {}, []
    swap_v = swap_start(dvw, part_v, pair_v, 0)

    for ref, k in wait_v:
        arrive(ref, k)
    window(gv, vsw)

    def weight_grads(a, i, sums):
        dp = dot_nt(vsw[a, key_rows(i), :], g_s[a])
        for g in range(GROUPS):
            cols = pl.ds(g * 128, 128)
            dpg = dp[:, g * 128:(g + 1) * 128]
            sbuf[a, key_rows(i), cols] = dpg
            sums[g] = sums[g] + fold8(pbuf[a, key_rows(i), cols].astype(F32) * dpg, jnp.sum)

    dsums = []
    for a in range(2):
        sums = [zero] * GROUPS
        for i in range(BLOCKS):
            weight_grads(a, i, sums)
        dsums += sums
    delta = [jnp.sum(t, axis=0, keepdims=True) * r for t, r in zip(dsums, inv_l)]

    scaled_queries()
    rs_v = scatter_rings(dvw, part_v, pair_v, sum_v, got_v, swap_v, 8)

    def grad_step(j, carry):
        rows = pl.ds(pl.multiple_of(j * KC, 16), KC)
        for a in range(2):
            for g in range(GROUPS):
                cols = pl.ds(g * 128, 128)
                pw = pbuf[a, rows, cols].astype(F32)
                dsbuf[a, rows, cols] = (pw * (sbuf[a, rows, cols] - delta[a * GROUPS + g])).astype(BF16)
            dkw[a, pl.ds(j * spans_of, spans_of)] = dot_nn(dsbuf[a, rows, :], qn_s[a]).reshape(spans_of, STRETCH, DIM)
        return carry

    lax.fori_loop(0, WROWS // KC, grad_step, 0)

    swap_k = swap_start(dkw, part_k, pair_k, 4)

    rs_k = scatter_rings(dkw, part_k, pair_k, sum_k, got_k, swap_k, 40)

    def turn_step(j, carry):
        rows = pl.ds(pl.multiple_of(j * 128, 128), 128)
        for a in range(2):
            ktw[a, :, rows] = ksw[a, rows, :].T
        return carry

    lax.fori_loop(0, WIN // 2, turn_step, 0)
    def queries_out():
        for a in range(2):
            dqt = dot_nn(ktw[a], dsbuf[a])
            for g in range(GROUPS):
                out = (dqt[:, g * 128:(g + 1) * 128] * (inv_l[a * GROUPS + g] * scale)).T.astype(BF16)
                for i in range(2):
                    dq_ref[pl.ds(a * STRETCH, STRETCH), pl.ds((2 * g + i) * DIM, DIM)] = out[i * STRETCH:(i + 1) * STRETCH]

    rs_v2 = scatter_rest(sum_v, got_v, mid_v, last_v, rs_v, 72)
    for cp in sent + list(swap_v.values()) + list(swap_k.values()) + list(rs_v.values()):
        cp.wait_send()
    queries_out()
    rs_k2 = scatter_rest(sum_k, got_k, mid_k, last_k, rs_k, 80)
    for cp in list(rs_k.values()) + rs_v2:
        cp.wait_send()
    collect_rest(mid_v, last_v, rs_v2, dv_ref)
    collect_rest(mid_k, last_k, rs_k2, dk_ref)
    for cp in rs_k2:
        cp.wait_send()


def copy_out(*refs):
    sem = refs[6]
    cps = [pltpu.make_async_copy(refs[i], refs[i + 3], sem.at[i]) for i in range(3)]
    for cp in cps:
        cp.start()
    for cp in cps:
        cp.wait()


def body(queries, keys, values, grad_out, doc_lengths, stretch_order):
    anyspec = pl.BlockSpec(memory_space=pl.ANY)
    smem = pl.BlockSpec(memory_space=pltpu.SMEM)
    vmem = pl.BlockSpec(memory_space=pltpu.VMEM)
    half = (STRETCH, DIM)
    outs = tuple(jax.ShapeDtypeStruct(s.shape, BF16) for s in (queries, keys, values))
    kept = tuple(pltpu.VMEM(s.shape, BF16) for s in outs)
    hbm = pl.BlockSpec(memory_space=pltpu.HBM)
    grads = pl.pallas_call(
        kernel,
        out_shape=kept,
        in_specs=[hbm] * 4 + [smem] * 2,
        out_specs=(vmem, vmem, vmem),
        scratch_shapes=[
            pltpu.VMEM((STRETCHES,) + half, BF16),
            pltpu.VMEM((STRETCHES,) + half, BF16),
            pltpu.VMEM((2 * STRETCH, HEADS * DIM), BF16),
            pltpu.VMEM((2 * STRETCH, HEADS * DIM), BF16),
            pltpu.VMEM((2, COLS, DIM), BF16),
            pltpu.VMEM((2, COLS, DIM), BF16),
            pltpu.VMEM((2, COLS, DIM), BF16),
            pltpu.VMEM((2, COLS, DIM), BF16),
            pltpu.VMEM((2, WROWS, DIM), BF16),
            pltpu.VMEM((2, WROWS, DIM), BF16),
            pltpu.VMEM((2, DIM, WROWS), BF16),
            pltpu.VMEM((2, WROWS, COLS), F32),
            pltpu.VMEM((2, WROWS, COLS), BF16),
            pltpu.VMEM((2, WROWS, COLS), BF16),
            pltpu.VMEM((2, WIN + 1) + half, F32),
            pltpu.VMEM((2, WIN + 1) + half, F32),
            pltpu.VMEM((2, RING, 2, RING) + half, BF16),
            pltpu.VMEM((2, RING, 2, RING) + half, BF16),
            pltpu.VMEM((RING, 2, RING) + half, BF16),
            pltpu.VMEM((RING, 2, RING) + half, BF16),
            pltpu.VMEM((RING, 2, RING) + half, BF16),
            pltpu.VMEM((RING, 2, RING) + half, BF16),
            pltpu.VMEM((RING, 2, RING) + half, BF16),
            pltpu.VMEM((RING, 2, RING) + half, BF16),
            pltpu.VMEM((2, RING) + half, BF16),
            pltpu.VMEM((2, RING) + half, BF16),
            pltpu.VMEM((2, RING) + half, BF16),
            pltpu.VMEM((2, RING) + half, BF16),
            pltpu.VMEM((8, 128), jnp.int32),
            pltpu.SMEM((8, 128), jnp.int32),
            pltpu.SemaphoreType.DMA((7,)),
            pltpu.SemaphoreType.DMA((N_AG,)),
            pltpu.SemaphoreType.DMA((N_AG,)),
            pltpu.SemaphoreType.DMA((N_RS,)),
            pltpu.SemaphoreType.DMA((N_RS,)),
        ],
        compiler_params=pltpu.CompilerParams(
            collective_id=0, has_side_effects=True, vmem_limit_bytes=58 * 1024 * 1024
        ),
    )(queries, keys, values, grad_out, doc_lengths, stretch_order)
    return pl.pallas_call(
        copy_out,
        out_shape=outs,
        in_specs=[vmem] * 3,
        out_specs=(hbm,) * 3,
        scratch_shapes=[pltpu.SemaphoreType.DMA((3,))],
    )(*(pltpu.with_memory_space_constraint(t, pltpu.VMEM) for t in grads))


def solution(mesh):
    return jax.shard_map(
        body,
        mesh=mesh,
        in_specs=(P("ctx", "head"), P("ctx", "head"), P("ctx", "head"), P("ctx", "head"), P(), P()),
        out_specs=(P("ctx", "head"), P("ctx", "head"), P("ctx", "head")),
        check_vma=False,
    )
```

```python
import functools

import jax
import jax.numpy as jnp
from jax import lax
from jax.experimental import pallas as pl
from jax.experimental.pallas import tpu as pltpu
from jax.sharding import PartitionSpec as P

MESH = pl.DeviceIdType.MESH
F32, BF16 = jnp.float32, jnp.bfloat16
RING = 4
CHIPS = RING * RING
HEADS, DIM = 8, 128
STRETCH = 64
STRETCHES = 64
COLS = HEADS * STRETCH
GROUPS = COLS // 128
WIN = 34
WROWS = WIN * STRETCH
KC = 1088
ROWS = 128
BLOCKS = WROWS // ROWS
WIDE = 272
WIDES = WROWS // WIDE
NEG = -1e30
N_AG = 128
N_RS = 96
HERE = 2


def dot_nt(a, b):
    return lax.dot_general(a, b, (((1,), (1,)), ((), ())), preferred_element_type=F32)


def dot_nn(a, b):
    return lax.dot_general(a, b, (((1,), (0,)), ((), ())), preferred_element_type=F32)


def fold8(v, op):
    return op(v.reshape(v.shape[0] // 8, 8, v.shape[1]), axis=0)


def kernel(
    q_hbm, k_hbm, v_hbm, g_hbm, len_ref, ord_ref,
    dq_ref, dk_ref, dv_ref,
    gk, gv, q_in, g_in, q_s, g_s, qn_s, gn_s, ksw, vsw, ktw, sbuf, pbuf, dsbuf, dkw, dvw,
    part_k, part_v, pair_k, pair_v, sum_k, sum_v, got_k, got_v, mid_k, mid_v, last_k, last_v, inv_vec, inv_ref,
    loc_sem, ag_send, ag_recv, rs_send, rs_recv,
):
    me = lax.axis_index("ctx")
    head = lax.axis_index("head")
    c = lax.rem(me, 2)
    x = lax.rem(lax.div(me, 2), RING)
    y = lax.div(me, 2 * RING)
    oc = 1 - c

    def wrap(v):
        return lax.rem(v, RING)

    xs = [wrap(x + d) for d in range(RING)]
    ys = [wrap(y + d) for d in range(RING)]
    x2, y2 = xs[2], ys[2]

    def dev(yy, xx, cc):
        return ((yy * RING + xx) * 2 + cc, head)

    sib = dev(y, x, oc)

    barrier = pltpu.get_barrier_semaphore()
    peers = [dev(y, xs[d], c) for d in (1, 2, 3)] + [dev(ys[d], x, c) for d in (1, 2, 3)] + [sib]
    for peer in peers:
        pl.semaphore_signal(barrier, inc=1, device_id=peer, device_id_type=MESH)
    own = []
    for i, (src, dst) in enumerate(((k_hbm, gk), (v_hbm, gv))):
        for h in range(2):
            rows = pl.ds(h * STRETCH, STRETCH)
            own.append(pltpu.make_async_copy(src.at[rows], dst.at[2 * me + h], loc_sem.at[2 * i + h]))
    loads = [
        pltpu.make_async_copy(q_hbm, q_in, loc_sem.at[4]),
        pltpu.make_async_copy(g_hbm, g_in, loc_sem.at[5]),
    ]
    for cp in own + loads:
        cp.start()

    pl.semaphore_wait(barrier, len(peers))

    sent = []
    count = [0]

    def send(ref, to):
        k = count[0]
        count[0] += 1
        cp = pltpu.make_async_remote_copy(
            src_ref=ref, dst_ref=ref, send_sem=ag_send.at[k], recv_sem=ag_recv.at[k],
            device_id=to, device_id_type=MESH,
        )
        cp.start()
        sent.append(cp)
        return k

    def arrive(ref, k):
        pltpu.make_async_remote_copy(
            src_ref=ref, dst_ref=ref, send_sem=ag_send.at[k], recv_sem=ag_recv.at[k],
            device_id=sib, device_id_type=MESH,
        ).wait_recv()

    def block(yy, xx, cc):
        return ((yy * RING + xx) * 2 + cc) * 2

    def node(buf, yy, xx, cc):
        return buf.at[pl.ds(block(yy, xx, cc), 2)]

    def part_of(buf, yy, xx, cc, half):
        return buf.at[block(yy, xx, cc) + half]

    far_first, near_first, group_order = (2, 1, 3), (1, 3, 2), (0, 1, 3, 2)

    def first_halves(buf):
        along_x = {d: send(part_of(buf, y, x, c, 0), dev(y, xs[d], c)) for d in far_first}
        along_y = {d: send(part_of(buf, y, x, c, 1), dev(ys[d], x, c)) for d in far_first}
        return along_x, along_y

    def other_halves(buf, pending):
        along_x = {d: send(part_of(buf, y, x, c, 1), dev(y, xs[d], c)) for d in far_first}
        along_y = {d: send(part_of(buf, y, x, c, 0), dev(ys[d], x, c)) for d in far_first}
        pending.append((node(buf, y, x, oc), send(node(buf, y, x, c), sib)))
        return along_x, along_y

    def second_stage(buf, along_x, along_y):
        coming = []
        for d in near_first:
            xx, yy = xs[RING - d], ys[RING - d]
            arrive(part_of(buf, y, xx, c, 0), along_x[d])
            for e in far_first:
                k = send(part_of(buf, y, xx, c, 0), dev(ys[e], x, c))
                coming.append((e, ys[RING - e], xx, 0, k))
            arrive(part_of(buf, yy, x, c, 1), along_y[d])
            for e in far_first:
                k = send(part_of(buf, yy, x, c, 1), dev(y, xs[e], c))
                coming.append((e, yy, xs[RING - e], 1, k))
        return coming

    def share_first(buf, along_x, along_y, pending):
        for d in near_first:
            xx, yy = xs[RING - d], ys[RING - d]
            arrive(part_of(buf, y, xx, c, 1), along_x[d])
            pending.append((node(buf, y, xx, oc), send(node(buf, y, xx, c), sib)))
            arrive(part_of(buf, yy, x, c, 0), along_y[d])
            pending.append((node(buf, yy, x, oc), send(node(buf, yy, x, c), sib)))

    def share_second(buf, coming, pending, which):
        for e in which:
            for ee, yy, xx, half, k in coming:
                if ee == e:
                    arrive(part_of(buf, yy, xx, c, half), k)
                    pending.append((part_of(buf, yy, xx, oc, half), send(part_of(buf, yy, xx, c, half), sib)))

    lane = lax.broadcasted_iota(jnp.int32, (8, 128), 1)

    def invert_order():
        inv = jnp.zeros((8, 128), jnp.int32)
        for b in range(STRETCHES):
            inv = jnp.where(lane == ord_ref[b], b, inv)
        inv_vec[...] = inv
        cp = pltpu.make_async_copy(inv_vec, inv_ref, loc_sem.at[6])
        cp.start()
        return cp

    def stack_heads():
        for cp in loads:
            cp.wait()
        for a in range(2):
            for h in range(HEADS):
                src = (pl.ds(a * STRETCH, STRETCH), pl.ds(h * DIM, DIM))
                q_s[a, pl.ds(h * STRETCH, STRETCH), :] = q_in[src]
                g_s[a, pl.ds(h * STRETCH, STRETCH), :] = g_in[src]

    wait_k, wait_v = [], []
    for cp in own[:2]:
        cp.wait()
    k1 = first_halves(gk)
    for cp in own[2:]:
        cp.wait()
    v1 = first_halves(gv)
    k1b = other_halves(gk, wait_k)
    v1b = other_halves(gv, wait_v)
    inv_copy = invert_order()
    k2 = second_stage(gk, *k1)
    v2 = second_stage(gv, *v1)
    share_first(gk, *k1b, wait_k)
    stack_heads()
    share_second(gk, k2, wait_k, near_first)
    share_first(gv, *v1b, wait_v)
    inv_copy.wait()

    spots, base = [], []
    for a in range(2):
        p = ord_ref[2 * me + a]
        spots.append(p)
        base.append(jnp.maximum(lax.div(p, 2) * 2 - 32, 0))

    scale = DIM ** -0.5
    log2e = 1.4426950408889634
    starts = [jnp.int32(0)]
    for d in range(3):
        starts.append(starts[-1] + len_ref[d])
    row_in = jnp.where(lane[:1] >= STRETCH, lane[:1] - STRETCH, lane[:1])
    pos_row, first_row = [], []
    for a in range(2):
        pr = spots[a] * STRETCH + row_in
        fr = jnp.zeros_like(pr)
        for st in starts:
            fr = jnp.maximum(fr, jnp.where(st <= pr, st, 0))
        pos_row.append(pr)
        first_row.append(fr)

    def window(src, dst):
        def step(w, carry):
            rows = pl.ds(pl.multiple_of(w * STRETCH, STRETCH), STRETCH)
            for a in range(2):
                dst[a, rows, :] = src[inv_ref[0, base[a] + w]]
            return carry

        lax.fori_loop(0, WIN, step, 0, unroll=17)

    for ref, k in wait_k:
        arrive(ref, k)
    window(gk, ksw)

    def key_rows(i):
        return pl.ds(i * ROWS, ROWS)

    def wide_rows(i):
        return pl.ds(i * WIDE, WIDE)

    def scores(a):
        tops = [jnp.full((8, 128), NEG, F32)] * GROUPS

        def raise_tops(i):
            for g in range(GROUPS):
                tops[g] = jnp.maximum(tops[g], fold8(sbuf[a, wide_rows(i), pl.ds(g * 128, 128)], jnp.max))

        for i in range(WIDES):
            s = dot_nt(ksw[a, wide_rows(i), :], q_s[a])
            kpos = base[a] * STRETCH + i * WIDE + lax.broadcasted_iota(jnp.int32, (WIDE, 128), 0)
            ok = (kpos <= pos_row[a]) & (kpos >= first_row[a])
            for g in range(GROUPS):
                sg = jnp.where(ok, s[:, g * 128:(g + 1) * 128] * (scale * log2e), NEG)
                sbuf[a, wide_rows(i), pl.ds(g * 128, 128)] = sg
            if i:
                raise_tops(i - 1)
        raise_tops(WIDES - 1)
        return [jnp.max(t, axis=0, keepdims=True) for t in tops]

    def weights(a, i, sums):
        for g in range(GROUPS):
            cols = pl.ds(g * 128, 128)
            pw = jnp.exp2(sbuf[a, wide_rows(i), cols] - tops[a][g])
            pbuf[a, wide_rows(i), cols] = pw.astype(BF16)
            sums[g] = sums[g] + fold8(pw, jnp.sum)

    def inverse_sums(a, sums):
        for g in range(GROUPS):
            inv_l.append(1.0 / jnp.sum(sums[g], axis=0, keepdims=True))

    def column(a, g):
        return jnp.broadcast_to(inv_l[a * GROUPS + g], (128, 128)).T

    def scaled_grads(a):
        for g in range(GROUPS):
            rows = pl.ds(g * 128, 128)
            gn_s[a, rows, :] = (g_s[a, rows, :].astype(F32) * column(a, g)).astype(BF16)

    def scaled_queries():
        for a in range(2):
            for g in range(GROUPS):
                rows = pl.ds(g * 128, 128)
                qn_s[a, rows, :] = (q_s[a, rows, :].astype(F32) * (column(a, g) * scale)).astype(BF16)

    def value_grads(a, i):
        part = dot_nn(pbuf[a, pl.ds(i * KC, KC), :], gn_s[a])
        dvw[a, pl.ds(i * spans_of, spans_of)] = part.reshape(spans_of, STRETCH, DIM)

    spans_of = KC // STRETCH
    zero = jnp.zeros((8, 128), F32)
    tops, inv_l = [], []
    for a in range(2):
        tops.append([jnp.zeros((1, 128), F32)] * GROUPS)
    tops[0] = scores(0)
    share_second(gv, v2, wait_v, near_first[:2])
    tops[1] = scores(1)
    share_second(gv, v2, wait_v, near_first[2:])
    sums = [zero] * GROUPS
    for i in range(WIDES):
        weights(0, i, sums)
    inverse_sums(0, sums)
    scaled_grads(0)
    sums = [zero] * GROUPS
    for i in range(WIDES):
        weights(1, i, sums)
    inverse_sums(1, sums)
    scaled_grads(1)
    for a in range(2):
        for i in range(WROWS // KC):
            value_grads(a, i)

    spans_of = KC // STRETCH

    def spare_blocks():
        for a in range(2):
            dkw[a, WIN] = jnp.zeros((STRETCH, DIM), F32)
            dvw[a, WIN] = jnp.zeros((STRETCH, DIM), F32)

    spare_blocks()

    def rs_copy(src, dst, k, to):
        return pltpu.make_async_remote_copy(
            src_ref=src, dst_ref=dst, send_sem=rs_send.at[k], recv_sem=rs_recv.at[k],
            device_id=to, device_id_type=MESH,
        )

    def unsort(w, part, cc, i):
        def step(g, carry):
            for half in range(2):
                dy, dx = (i, g) if half == 0 else (g, i)
                chip = wrap(y + 2 + dy) * RING + wrap(x + 2 + dx)
                s = ord_ref[2 * (2 * chip + cc) + half]
                at = []
                for a in range(2):
                    off = s - base[a]
                    at.append(jnp.where((off >= 0) & (off < WIN), off, WIN))
                part[cc, i, half, g] = (w[0, at[0]] + w[1, at[1]]).astype(BF16)
            return carry

        lax.fori_loop(0, RING, step, 0, unroll=True)

    def swap_start(w, part, pair, k0):
        cps = {}
        for i in group_order:
            unsort(w, part, oc, i)
            cps[i] = rs_copy(part.at[oc, i], pair.at[i], k0 + i, sib)
            cps[i].start()
        return cps

    def ring_peer(half, g):
        return dev(y, xs[(2 + g) % RING], c) if half == 0 else dev(ys[(2 + g) % RING], x, c)

    def scatter_rings(w, part, pair, total, got, cps, k0):
        out = {}
        for i in group_order:
            unsort(w, part, c, i)
            cps[i].wait_recv()
            for g in group_order:
                for half in range(2):
                    both = part[c, i, half, g].astype(F32) + pair[i, half, g].astype(F32)
                    total[i, half, g] = both.astype(BF16)
                    if g != HERE:
                        k = k0 + (i * 2 + half) * RING + g
                        cp = rs_copy(total.at[i, half, g], got.at[i, half, g], k, ring_peer(half, g))
                        cp.start()
                        out[i, half, g] = cp
        return out

    def scatter_rest(total, got, mid, last, cps, k0):
        out = []
        for i in group_order:
            for half in range(2):
                acc = total[i, half, HERE].astype(F32)
                for g in group_order[:3]:
                    cps[i, half, g].wait_recv()
                    acc = acc + got[i, half, g].astype(F32)
                mid[half, i] = acc.astype(BF16)
                if i != HERE:
                    cp = rs_copy(mid.at[half, i], last.at[half, i], k0 + 2 * i + half, ring_peer(1 - half, i))
                    cp.start()
                    out.append(cp)
        return out

    def collect_rest(mid, last, cps, out):
        for cp in cps:
            cp.wait_recv()
        for half in range(2):
            acc = mid[half, HERE].astype(F32)
            for i in group_order[:3]:
                acc = acc + last[half, i].astype(F32)
            out[pl.ds(half * STRETCH, STRETCH), :] = acc.astype(BF16)

    swap_v, swap_k, rs_v, rs_v2, rs_k, rs_k2 = {}, {}, {}, [], {}, []
    swap_v = swap_start(dvw, part_v, pair_v, 0)

    for ref, k in wait_v:
        arrive(ref, k)
    window(gv, vsw)

    def weight_grads(a, i, sums):
        dp = dot_nt(vsw[a, wide_rows(i), :], g_s[a])
        for g in range(GROUPS):
            cols = pl.ds(g * 128, 128)
            dpg = dp[:, g * 128:(g + 1) * 128]
            sbuf[a, wide_rows(i), cols] = dpg
            sums[g] = sums[g] + fold8(pbuf[a, wide_rows(i), cols].astype(F32) * dpg, jnp.sum)

    dsums = []
    for a in range(2):
        sums = [zero] * GROUPS
        for i in range(WIDES):
            weight_grads(a, i, sums)
        dsums += sums
    delta = [jnp.sum(t, axis=0, keepdims=True) * r for t, r in zip(dsums, inv_l)]

    scaled_queries()
    rs_v = scatter_rings(dvw, part_v, pair_v, sum_v, got_v, swap_v, 8)

    def grad_step(j, carry):
        rows = pl.ds(pl.multiple_of(j * KC, 16), KC)
        for a in range(2):
            for g in range(GROUPS):
                cols = pl.ds(g * 128, 128)
                pw = pbuf[a, rows, cols].astype(F32)
                dsbuf[a, rows, cols] = (pw * (sbuf[a, rows, cols] - delta[a * GROUPS + g])).astype(BF16)
            dkw[a, pl.ds(j * spans_of, spans_of)] = dot_nn(dsbuf[a, rows, :], qn_s[a]).reshape(spans_of, STRETCH, DIM)
        return carry

    lax.fori_loop(0, WROWS // KC, grad_step, 0)

    swap_k = swap_start(dkw, part_k, pair_k, 4)

    rs_k = scatter_rings(dkw, part_k, pair_k, sum_k, got_k, swap_k, 40)

    def turn_step(j, carry):
        rows = pl.ds(pl.multiple_of(j * 128, 128), 128)
        for a in range(2):
            ktw[a, :, rows] = ksw[a, rows, :].T
        return carry

    lax.fori_loop(0, WIN // 2, turn_step, 0)
    def queries_out():
        for a in range(2):
            dqt = dot_nn(ktw[a], dsbuf[a])
            for g in range(GROUPS):
                out = (dqt[:, g * 128:(g + 1) * 128] * (inv_l[a * GROUPS + g] * scale)).T.astype(BF16)
                for i in range(2):
                    dq_ref[pl.ds(a * STRETCH, STRETCH), pl.ds((2 * g + i) * DIM, DIM)] = out[i * STRETCH:(i + 1) * STRETCH]

    rs_v2 = scatter_rest(sum_v, got_v, mid_v, last_v, rs_v, 72)
    for cp in sent + list(swap_v.values()) + list(swap_k.values()) + list(rs_v.values()):
        cp.wait_send()
    queries_out()
    rs_k2 = scatter_rest(sum_k, got_k, mid_k, last_k, rs_k, 80)
    for cp in list(rs_k.values()) + rs_v2:
        cp.wait_send()
    collect_rest(mid_v, last_v, rs_v2, dv_ref)
    collect_rest(mid_k, last_k, rs_k2, dk_ref)
    for cp in rs_k2:
        cp.wait_send()


def copy_out(*refs):
    sem = refs[6]
    cps = [pltpu.make_async_copy(refs[i], refs[i + 3], sem.at[i]) for i in range(3)]
    for cp in cps:
        cp.start()
    for cp in cps:
        cp.wait()


def body(queries, keys, values, grad_out, doc_lengths, stretch_order):
    anyspec = pl.BlockSpec(memory_space=pl.ANY)
    smem = pl.BlockSpec(memory_space=pltpu.SMEM)
    vmem = pl.BlockSpec(memory_space=pltpu.VMEM)
    half = (STRETCH, DIM)
    outs = tuple(jax.ShapeDtypeStruct(s.shape, BF16) for s in (queries, keys, values))
    kept = tuple(pltpu.VMEM(s.shape, BF16) for s in outs)
    hbm = pl.BlockSpec(memory_space=pltpu.HBM)
    grads = pl.pallas_call(
        kernel,
        out_shape=kept,
        in_specs=[hbm] * 4 + [smem] * 2,
        out_specs=(vmem, vmem, vmem),
        scratch_shapes=[
            pltpu.VMEM((STRETCHES,) + half, BF16),
            pltpu.VMEM((STRETCHES,) + half, BF16),
            pltpu.VMEM((2 * STRETCH, HEADS * DIM), BF16),
            pltpu.VMEM((2 * STRETCH, HEADS * DIM), BF16),
            pltpu.VMEM((2, COLS, DIM), BF16),
            pltpu.VMEM((2, COLS, DIM), BF16),
            pltpu.VMEM((2, COLS, DIM), BF16),
            pltpu.VMEM((2, COLS, DIM), BF16),
            pltpu.VMEM((2, WROWS, DIM), BF16),
            pltpu.VMEM((2, WROWS, DIM), BF16),
            pltpu.VMEM((2, DIM, WROWS), BF16),
            pltpu.VMEM((2, WROWS, COLS), F32),
            pltpu.VMEM((2, WROWS, COLS), BF16),
            pltpu.VMEM((2, WROWS, COLS), BF16),
            pltpu.VMEM((2, WIN + 1) + half, F32),
            pltpu.VMEM((2, WIN + 1) + half, F32),
            pltpu.VMEM((2, RING, 2, RING) + half, BF16),
            pltpu.VMEM((2, RING, 2, RING) + half, BF16),
            pltpu.VMEM((RING, 2, RING) + half, BF16),
            pltpu.VMEM((RING, 2, RING) + half, BF16),
            pltpu.VMEM((RING, 2, RING) + half, BF16),
            pltpu.VMEM((RING, 2, RING) + half, BF16),
            pltpu.VMEM((RING, 2, RING) + half, BF16),
            pltpu.VMEM((RING, 2, RING) + half, BF16),
            pltpu.VMEM((2, RING) + half, BF16),
            pltpu.VMEM((2, RING) + half, BF16),
            pltpu.VMEM((2, RING) + half, BF16),
            pltpu.VMEM((2, RING) + half, BF16),
            pltpu.VMEM((8, 128), jnp.int32),
            pltpu.SMEM((8, 128), jnp.int32),
            pltpu.SemaphoreType.DMA((7,)),
            pltpu.SemaphoreType.DMA((N_AG,)),
            pltpu.SemaphoreType.DMA((N_AG,)),
            pltpu.SemaphoreType.DMA((N_RS,)),
            pltpu.SemaphoreType.DMA((N_RS,)),
        ],
        compiler_params=pltpu.CompilerParams(
            collective_id=0, has_side_effects=True, vmem_limit_bytes=58 * 1024 * 1024
        ),
    )(queries, keys, values, grad_out, doc_lengths, stretch_order)
    return pl.pallas_call(
        copy_out,
        out_shape=outs,
        in_specs=[vmem] * 3,
        out_specs=(hbm,) * 3,
        scratch_shapes=[pltpu.SemaphoreType.DMA((3,))],
    )(*(pltpu.with_memory_space_constraint(t, pltpu.VMEM) for t in grads))


def solution(mesh):
    return jax.shard_map(
        body,
        mesh=mesh,
        in_specs=(P("ctx", "head"), P("ctx", "head"), P("ctx", "head"), P("ctx", "head"), P(), P()),
        out_specs=(P("ctx", "head"), P("ctx", "head"), P("ctx", "head")),
        check_vma=False,
    )
```

```python
import functools

import jax
import jax.numpy as jnp
from jax import lax
from jax.experimental import pallas as pl
from jax.experimental.pallas import tpu as pltpu
from jax.sharding import PartitionSpec as P

MESH = pl.DeviceIdType.MESH
F32, BF16 = jnp.float32, jnp.bfloat16
RING = 4
CHIPS = RING * RING
HEADS, DIM = 8, 128
STRETCH = 64
STRETCHES = 64
COLS = HEADS * STRETCH
GROUPS = COLS // 128
WIN = 34
WROWS = WIN * STRETCH
KC = 1088
ROWS = 128
BLOCKS = WROWS // ROWS
WIDE = 272
WIDES = WROWS // WIDE
NEG = -1e30
N_AG = 128
N_RS = 96
HERE = 2


def dot_nt(a, b):
    return lax.dot_general(a, b, (((1,), (1,)), ((), ())), preferred_element_type=F32)


def dot_nn(a, b):
    return lax.dot_general(a, b, (((1,), (0,)), ((), ())), preferred_element_type=F32)


def fold8(v, op):
    return op(v.reshape(v.shape[0] // 8, 8, v.shape[1]), axis=0)


def kernel(
    q_hbm, k_hbm, v_hbm, g_hbm, len_ref, ord_ref,
    dq_ref, dk_ref, dv_ref,
    gk, gv, q_in, g_in, q_s, g_s, qn_s, gn_s, ksw, vsw, ktw, sbuf, pbuf, dsbuf, dkw, dvw,
    part_k, part_v, pair_k, pair_v, sum_k, sum_v, got_k, got_v, mid_k, mid_v, last_k, last_v, inv_vec, inv_ref,
    loc_sem, ag_send, ag_recv, rs_send, rs_recv,
):
    me = lax.axis_index("ctx")
    head = lax.axis_index("head")
    c = lax.rem(me, 2)
    x = lax.rem(lax.div(me, 2), RING)
    y = lax.div(me, 2 * RING)
    oc = 1 - c

    def wrap(v):
        return lax.rem(v, RING)

    xs = [wrap(x + d) for d in range(RING)]
    ys = [wrap(y + d) for d in range(RING)]
    x2, y2 = xs[2], ys[2]

    def dev(yy, xx, cc):
        return ((yy * RING + xx) * 2 + cc, head)

    sib = dev(y, x, oc)

    barrier = pltpu.get_barrier_semaphore()
    peers = [dev(y, xs[d], c) for d in (1, 2, 3)] + [dev(ys[d], x, c) for d in (1, 2, 3)] + [sib]
    for peer in peers:
        pl.semaphore_signal(barrier, inc=1, device_id=peer, device_id_type=MESH)
    own = []
    for i, (src, dst) in enumerate(((k_hbm, gk), (v_hbm, gv))):
        for h in range(2):
            rows = pl.ds(h * STRETCH, STRETCH)
            own.append(pltpu.make_async_copy(src.at[rows], dst.at[2 * me + h], loc_sem.at[2 * i + h]))
    loads = [
        pltpu.make_async_copy(q_hbm, q_in, loc_sem.at[4]),
        pltpu.make_async_copy(g_hbm, g_in, loc_sem.at[5]),
    ]
    for cp in own + loads:
        cp.start()

    pl.semaphore_wait(barrier, len(peers))

    sent = []
    count = [0]

    def send(ref, to):
        k = count[0]
        count[0] += 1
        cp = pltpu.make_async_remote_copy(
            src_ref=ref, dst_ref=ref, send_sem=ag_send.at[k], recv_sem=ag_recv.at[k],
            device_id=to, device_id_type=MESH,
        )
        cp.start()
        sent.append(cp)
        return k

    def arrive(ref, k):
        pltpu.make_async_remote_copy(
            src_ref=ref, dst_ref=ref, send_sem=ag_send.at[k], recv_sem=ag_recv.at[k],
            device_id=sib, device_id_type=MESH,
        ).wait_recv()

    def block(yy, xx, cc):
        return ((yy * RING + xx) * 2 + cc) * 2

    def node(buf, yy, xx, cc):
        return buf.at[pl.ds(block(yy, xx, cc), 2)]

    def part_of(buf, yy, xx, cc, half):
        return buf.at[block(yy, xx, cc) + half]

    far_first, near_first, group_order = (2, 1, 3), (1, 3, 2), (0, 1, 3, 2)

    def first_halves(buf):
        along_x = {d: send(part_of(buf, y, x, c, 0), dev(y, xs[d], c)) for d in far_first}
        along_y = {d: send(part_of(buf, y, x, c, 1), dev(ys[d], x, c)) for d in far_first}
        return along_x, along_y

    def other_halves(buf, pending):
        along_x = {d: send(part_of(buf, y, x, c, 1), dev(y, xs[d], c)) for d in far_first}
        along_y = {d: send(part_of(buf, y, x, c, 0), dev(ys[d], x, c)) for d in far_first}
        pending.append((node(buf, y, x, oc), send(node(buf, y, x, c), sib)))
        return along_x, along_y

    def second_stage(buf, along_x, along_y):
        coming = []
        for d in near_first:
            xx, yy = xs[RING - d], ys[RING - d]
            arrive(part_of(buf, y, xx, c, 0), along_x[d])
            for e in far_first:
                k = send(part_of(buf, y, xx, c, 0), dev(ys[e], x, c))
                coming.append((e, ys[RING - e], xx, 0, k))
            arrive(part_of(buf, yy, x, c, 1), along_y[d])
            for e in far_first:
                k = send(part_of(buf, yy, x, c, 1), dev(y, xs[e], c))
                coming.append((e, yy, xs[RING - e], 1, k))
        return coming

    def share_first(buf, along_x, along_y, pending):
        for d in near_first:
            xx, yy = xs[RING - d], ys[RING - d]
            arrive(part_of(buf, y, xx, c, 1), along_x[d])
            pending.append((node(buf, y, xx, oc), send(node(buf, y, xx, c), sib)))
            arrive(part_of(buf, yy, x, c, 0), along_y[d])
            pending.append((node(buf, yy, x, oc), send(node(buf, yy, x, c), sib)))

    def share_second(buf, coming, pending, which):
        for e in which:
            for ee, yy, xx, half, k in coming:
                if ee == e:
                    arrive(part_of(buf, yy, xx, c, half), k)
                    pending.append((part_of(buf, yy, xx, oc, half), send(part_of(buf, yy, xx, c, half), sib)))

    lane = lax.broadcasted_iota(jnp.int32, (8, 128), 1)

    def invert_order():
        inv = jnp.zeros((8, 128), jnp.int32)
        for b in range(STRETCHES):
            inv = jnp.where(lane == ord_ref[b], b, inv)
        inv_vec[...] = inv
        cp = pltpu.make_async_copy(inv_vec, inv_ref, loc_sem.at[6])
        cp.start()
        return cp

    def stack_heads():
        for cp in loads:
            cp.wait()
        for a in range(2):
            for h in range(HEADS):
                src = (pl.ds(a * STRETCH, STRETCH), pl.ds(h * DIM, DIM))
                q_s[a, pl.ds(h * STRETCH, STRETCH), :] = q_in[src]
                g_s[a, pl.ds(h * STRETCH, STRETCH), :] = g_in[src]

    wait_k, wait_v = [], []
    for cp in own[:2]:
        cp.wait()
    k1 = first_halves(gk)
    for cp in own[2:]:
        cp.wait()
    v1 = first_halves(gv)
    k1b = other_halves(gk, wait_k)
    v1b = other_halves(gv, wait_v)
    inv_copy = invert_order()
    k2 = second_stage(gk, *k1)
    v2 = second_stage(gv, *v1)
    share_first(gk, *k1b, wait_k)
    stack_heads()
    share_second(gk, k2, wait_k, near_first)
    share_first(gv, *v1b, wait_v)
    inv_copy.wait()

    spots, base = [], []
    for a in range(2):
        p = ord_ref[2 * me + a]
        spots.append(p)
        base.append(jnp.maximum(lax.div(p, 2) * 2 - 32, 0))

    scale = DIM ** -0.5
    log2e = 1.4426950408889634
    starts = [jnp.int32(0)]
    for d in range(3):
        starts.append(starts[-1] + len_ref[d])
    row_in = jnp.where(lane[:1] >= STRETCH, lane[:1] - STRETCH, lane[:1])
    pos_row, first_row = [], []
    for a in range(2):
        pr = spots[a] * STRETCH + row_in
        fr = jnp.zeros_like(pr)
        for st in starts:
            fr = jnp.maximum(fr, jnp.where(st <= pr, st, 0))
        pos_row.append(pr)
        first_row.append(fr)

    def window(src, dst):
        def step(w, carry):
            rows = pl.ds(pl.multiple_of(w * STRETCH, STRETCH), STRETCH)
            for a in range(2):
                dst[a, rows, :] = src[inv_ref[0, base[a] + w]]
            return carry

        lax.fori_loop(0, WIN, step, 0, unroll=17)

    for ref, k in wait_k:
        arrive(ref, k)
    window(gk, ksw)

    def key_rows(i):
        return pl.ds(i * ROWS, ROWS)

    def wide_rows(i):
        return pl.ds(i * WIDE, WIDE)

    def scores(a):
        tops = [jnp.full((8, 128), NEG, F32)] * GROUPS

        def raise_tops(i):
            for g in range(GROUPS):
                tops[g] = jnp.maximum(tops[g], fold8(sbuf[a, wide_rows(i), pl.ds(g * 128, 128)], jnp.max))

        for i in range(WIDES):
            s = dot_nt(ksw[a, wide_rows(i), :], q_s[a])
            kpos = base[a] * STRETCH + i * WIDE + lax.broadcasted_iota(jnp.int32, (WIDE, 128), 0)
            ok = (kpos <= pos_row[a]) & (kpos >= first_row[a])
            for g in range(GROUPS):
                sg = jnp.where(ok, s[:, g * 128:(g + 1) * 128] * (scale * log2e), NEG)
                sbuf[a, wide_rows(i), pl.ds(g * 128, 128)] = sg
            if i:
                raise_tops(i - 1)
        raise_tops(WIDES - 1)
        return [jnp.max(t, axis=0, keepdims=True) for t in tops]

    def weights(a, i, sums):
        for g in range(GROUPS):
            cols = pl.ds(g * 128, 128)
            pw = jnp.exp2(sbuf[a, wide_rows(i), cols] - tops[a][g])
            pbuf[a, wide_rows(i), cols] = pw.astype(BF16)
            sums[g] = sums[g] + fold8(pw, jnp.sum)

    def inverse_sums(a, sums):
        for g in range(GROUPS):
            inv_l.append(1.0 / jnp.sum(sums[g], axis=0, keepdims=True))

    def column(a, g):
        return jnp.broadcast_to(inv_l[a * GROUPS + g], (128, 128)).T

    def scaled_grads(a):
        for g in range(GROUPS):
            rows = pl.ds(g * 128, 128)
            gn_s[a, rows, :] = (g_s[a, rows, :].astype(F32) * column(a, g)).astype(BF16)

    def scaled_queries():
        for a in range(2):
            for g in range(GROUPS):
                rows = pl.ds(g * 128, 128)
                qn_s[a, rows, :] = (q_s[a, rows, :].astype(F32) * (column(a, g) * scale)).astype(BF16)

    def value_grads(a, i):
        part = dot_nn(pbuf[a, pl.ds(i * KC, KC), :], gn_s[a])
        dvw[a, pl.ds(i * spans_of, spans_of)] = part.reshape(spans_of, STRETCH, DIM)

    spans_of = KC // STRETCH
    zero = jnp.zeros((8, 128), F32)
    tops, inv_l = [], []
    for a in range(2):
        tops.append([jnp.zeros((1, 128), F32)] * GROUPS)
    tops[0] = scores(0)
    share_second(gv, v2, wait_v, near_first[:2])
    tops[1] = scores(1)
    share_second(gv, v2, wait_v, near_first[2:])
    sums = [zero] * GROUPS
    for i in range(WIDES):
        weights(0, i, sums)
    inverse_sums(0, sums)
    scaled_grads(0)
    sums = [zero] * GROUPS
    for i in range(WIDES):
        weights(1, i, sums)
    inverse_sums(1, sums)
    scaled_grads(1)
    for a in range(2):
        for i in range(WROWS // KC):
            value_grads(a, i)

    spans_of = KC // STRETCH

    def spare_blocks():
        for a in range(2):
            dkw[a, WIN] = jnp.zeros((STRETCH, DIM), F32)
            dvw[a, WIN] = jnp.zeros((STRETCH, DIM), F32)

    spare_blocks()

    def rs_copy(src, dst, k, to):
        return pltpu.make_async_remote_copy(
            src_ref=src, dst_ref=dst, send_sem=rs_send.at[k], recv_sem=rs_recv.at[k],
            device_id=to, device_id_type=MESH,
        )

    def unsort(w, part, cc, i):
        def step(g, carry):
            for half in range(2):
                dy, dx = (i, g) if half == 0 else (g, i)
                chip = wrap(y + 2 + dy) * RING + wrap(x + 2 + dx)
                s = ord_ref[2 * (2 * chip + cc) + half]
                at = []
                for a in range(2):
                    off = s - base[a]
                    at.append(jnp.where((off >= 0) & (off < WIN), off, WIN))
                part[cc, i, half, g] = (w[0, at[0]] + w[1, at[1]]).astype(BF16)
            return carry

        lax.fori_loop(0, RING, step, 0, unroll=True)

    def swap_start(w, part, pair, k0):
        cps = {}
        for i in group_order:
            unsort(w, part, oc, i)
            cps[i] = rs_copy(part.at[oc, i], pair.at[i], k0 + i, sib)
            cps[i].start()
        return cps

    def ring_peer(half, g):
        return dev(y, xs[(2 + g) % RING], c) if half == 0 else dev(ys[(2 + g) % RING], x, c)

    def scatter_rings(w, part, pair, total, got, cps, k0):
        out = {}
        for i in group_order:
            unsort(w, part, c, i)
            cps[i].wait_recv()
            for g in group_order:
                for half in range(2):
                    both = part[c, i, half, g].astype(F32) + pair[i, half, g].astype(F32)
                    total[i, half, g] = both.astype(BF16)
                    if g != HERE:
                        k = k0 + (i * 2 + half) * RING + g
                        cp = rs_copy(total.at[i, half, g], got.at[i, half, g], k, ring_peer(half, g))
                        cp.start()
                        out[i, half, g] = cp
        return out

    def scatter_rest(total, got, mid, last, cps, k0):
        out = []
        for i in group_order:
            for half in range(2):
                acc = total[i, half, HERE].astype(F32)
                for g in group_order[:3]:
                    cps[i, half, g].wait_recv()
                    acc = acc + got[i, half, g].astype(F32)
                mid[half, i] = acc.astype(BF16)
                if i != HERE:
                    cp = rs_copy(mid.at[half, i], last.at[half, i], k0 + 2 * i + half, ring_peer(1 - half, i))
                    cp.start()
                    out.append(cp)
        return out

    def collect_rest(mid, last, cps, out):
        for cp in cps:
            cp.wait_recv()
        for half in range(2):
            acc = mid[half, HERE].astype(F32)
            for i in group_order[:3]:
                acc = acc + last[half, i].astype(F32)
            out[pl.ds(half * STRETCH, STRETCH), :] = acc.astype(BF16)

    swap_v, swap_k, rs_v, rs_v2, rs_k, rs_k2 = {}, {}, {}, [], {}, []
    swap_v = swap_start(dvw, part_v, pair_v, 0)

    for ref, k in wait_v:
        arrive(ref, k)
    window(gv, vsw)

    def weight_grads(a, i, sums):
        dp = dot_nt(vsw[a, wide_rows(i), :], g_s[a])
        for g in range(GROUPS):
            cols = pl.ds(g * 128, 128)
            dpg = dp[:, g * 128:(g + 1) * 128]
            sbuf[a, wide_rows(i), cols] = dpg
            sums[g] = sums[g] + fold8(pbuf[a, wide_rows(i), cols].astype(F32) * dpg, jnp.sum)

    dsums = []
    for a in range(2):
        sums = [zero] * GROUPS
        for i in range(WIDES):
            weight_grads(a, i, sums)
        dsums += sums
    delta = [jnp.sum(t, axis=0, keepdims=True) * r for t, r in zip(dsums, inv_l)]

    scaled_queries()
    rs_v = scatter_rings(dvw, part_v, pair_v, sum_v, got_v, swap_v, 8)

    def grad_step(j, carry):
        rows = pl.ds(pl.multiple_of(j * KC, 16), KC)
        for a in range(2):
            for g in range(GROUPS):
                cols = pl.ds(g * 128, 128)
                pw = pbuf[a, rows, cols].astype(F32)
                dsbuf[a, rows, cols] = (pw * (sbuf[a, rows, cols] - delta[a * GROUPS + g])).astype(BF16)
            dkw[a, pl.ds(j * spans_of, spans_of)] = dot_nn(dsbuf[a, rows, :], qn_s[a]).reshape(spans_of, STRETCH, DIM)
        return carry

    lax.fori_loop(0, WROWS // KC, grad_step, 0, unroll=True)

    swap_k = swap_start(dkw, part_k, pair_k, 4)

    rs_k = scatter_rings(dkw, part_k, pair_k, sum_k, got_k, swap_k, 40)

    def turn_step(j, carry):
        rows = pl.ds(pl.multiple_of(j * 128, 128), 128)
        for a in range(2):
            ktw[a, :, rows] = ksw[a, rows, :].T
        return carry

    lax.fori_loop(0, WIN // 2, turn_step, 0)
    def queries_out():
        for a in range(2):
            dqt = dot_nn(ktw[a], dsbuf[a])
            for g in range(GROUPS):
                out = (dqt[:, g * 128:(g + 1) * 128] * (inv_l[a * GROUPS + g] * scale)).T.astype(BF16)
                for i in range(2):
                    dq_ref[pl.ds(a * STRETCH, STRETCH), pl.ds((2 * g + i) * DIM, DIM)] = out[i * STRETCH:(i + 1) * STRETCH]

    rs_v2 = scatter_rest(sum_v, got_v, mid_v, last_v, rs_v, 72)
    for cp in sent + list(swap_v.values()) + list(swap_k.values()) + list(rs_v.values()):
        cp.wait_send()
    queries_out()
    rs_k2 = scatter_rest(sum_k, got_k, mid_k, last_k, rs_k, 80)
    for cp in list(rs_k.values()) + rs_v2:
        cp.wait_send()
    collect_rest(mid_v, last_v, rs_v2, dv_ref)
    collect_rest(mid_k, last_k, rs_k2, dk_ref)
    for cp in rs_k2:
        cp.wait_send()


def copy_out(*refs):
    sem = refs[6]
    cps = [pltpu.make_async_copy(refs[i], refs[i + 3], sem.at[i]) for i in range(3)]
    for cp in cps:
        cp.start()
    for cp in cps:
        cp.wait()


def body(queries, keys, values, grad_out, doc_lengths, stretch_order):
    anyspec = pl.BlockSpec(memory_space=pl.ANY)
    smem = pl.BlockSpec(memory_space=pltpu.SMEM)
    vmem = pl.BlockSpec(memory_space=pltpu.VMEM)
    half = (STRETCH, DIM)
    outs = tuple(jax.ShapeDtypeStruct(s.shape, BF16) for s in (queries, keys, values))
    kept = tuple(pltpu.VMEM(s.shape, BF16) for s in outs)
    hbm = pl.BlockSpec(memory_space=pltpu.HBM)
    grads = pl.pallas_call(
        kernel,
        out_shape=kept,
        in_specs=[hbm] * 4 + [smem] * 2,
        out_specs=(vmem, vmem, vmem),
        scratch_shapes=[
            pltpu.VMEM((STRETCHES,) + half, BF16),
            pltpu.VMEM((STRETCHES,) + half, BF16),
            pltpu.VMEM((2 * STRETCH, HEADS * DIM), BF16),
            pltpu.VMEM((2 * STRETCH, HEADS * DIM), BF16),
            pltpu.VMEM((2, COLS, DIM), BF16),
            pltpu.VMEM((2, COLS, DIM), BF16),
            pltpu.VMEM((2, COLS, DIM), BF16),
            pltpu.VMEM((2, COLS, DIM), BF16),
            pltpu.VMEM((2, WROWS, DIM), BF16),
            pltpu.VMEM((2, WROWS, DIM), BF16),
            pltpu.VMEM((2, DIM, WROWS), BF16),
            pltpu.VMEM((2, WROWS, COLS), F32),
            pltpu.VMEM((2, WROWS, COLS), BF16),
            pltpu.VMEM((2, WROWS, COLS), BF16),
            pltpu.VMEM((2, WIN + 1) + half, F32),
            pltpu.VMEM((2, WIN + 1) + half, F32),
            pltpu.VMEM((2, RING, 2, RING) + half, BF16),
            pltpu.VMEM((2, RING, 2, RING) + half, BF16),
            pltpu.VMEM((RING, 2, RING) + half, BF16),
            pltpu.VMEM((RING, 2, RING) + half, BF16),
            pltpu.VMEM((RING, 2, RING) + half, BF16),
            pltpu.VMEM((RING, 2, RING) + half, BF16),
            pltpu.VMEM((RING, 2, RING) + half, BF16),
            pltpu.VMEM((RING, 2, RING) + half, BF16),
            pltpu.VMEM((2, RING) + half, BF16),
            pltpu.VMEM((2, RING) + half, BF16),
            pltpu.VMEM((2, RING) + half, BF16),
            pltpu.VMEM((2, RING) + half, BF16),
            pltpu.VMEM((8, 128), jnp.int32),
            pltpu.SMEM((8, 128), jnp.int32),
            pltpu.SemaphoreType.DMA((7,)),
            pltpu.SemaphoreType.DMA((N_AG,)),
            pltpu.SemaphoreType.DMA((N_AG,)),
            pltpu.SemaphoreType.DMA((N_RS,)),
            pltpu.SemaphoreType.DMA((N_RS,)),
        ],
        compiler_params=pltpu.CompilerParams(
            collective_id=0, has_side_effects=True, vmem_limit_bytes=58 * 1024 * 1024
        ),
    )(queries, keys, values, grad_out, doc_lengths, stretch_order)
    return pl.pallas_call(
        copy_out,
        out_shape=outs,
        in_specs=[vmem] * 3,
        out_specs=(hbm,) * 3,
        scratch_shapes=[pltpu.SemaphoreType.DMA((3,))],
    )(*(pltpu.with_memory_space_constraint(t, pltpu.VMEM) for t in grads))


def solution(mesh):
    return jax.shard_map(
        body,
        mesh=mesh,
        in_specs=(P("ctx", "head"), P("ctx", "head"), P("ctx", "head"), P("ctx", "head"), P(), P()),
        out_specs=(P("ctx", "head"), P("ctx", "head"), P("ctx", "head")),
        check_vma=False,
    )
```
